256 devices in a mesh: con: 16 (over z_hi, x, core), res: 16 (over y, z_lo).
Axes of the slice: x: 4, y: 4, z: 8 (z_hi: 2, z_lo: 4; z = z_hi * 4 + z_lo), core: 2. Of those that a mesh axis runs over, the one named last changes fastest.
Arguments:
- integrals: float32 [24576, 24576], P('res', 'con'), as said below
- tile_mask: int32 [96, 96], P('res', 'con'), may hold values from 0 to 1, as said below
- amplitudes: float32 [24576, 384], P(('con', 'res')), may hold values from -4 to 4
- other_first: float32 [24576, 384], P(('res', 'con')), may hold values from -6 to 6
- other_second: float32 [24576, 384], P(('con', 'res')), may hold values from -6 to 6
- vir_index: int32 [2, 24576], replicated, may hold values from 0 to 1599
- occ_index: int32 [2, 384], replicated, may hold values from 0 to 31, as said below
- partner: int32 [384], replicated, may hold values from 0 to 383, as said below
- eps_vir: float32 [1600], replicated, may hold values from 0.2 to 3
- eps_occ: float32 [32], replicated, may hold values from -2 to -0.2
Outputs:
- first_update: float32 [24576, 384], P(('res', 'con'))
- second_update: float32 [24576, 384], P(('con', 'res'))
The draws below stay inside these ranges and needn't reach their ends.
Inputs may be any that keep to these rules, and one draw needn't show every extreme that they name: integrals is symmetric: integrals[p, s] == integrals[s, p]. tile_mask is symmetric and its diagonal is 1. partner is a permutation that is its own inverse with no fixed point. The two orbitals of an occupied pair differ, and occ_index[0, partner[q]] == occ_index[1, q].
All inputs are finite; a program needn't handle non-finite values.
Results may differ from the reference program's by a relative error of at most 0.000065.
Values sent between devices are 32-bit elements; how exact they have to be, the bound alone decides.
A program may use at most 128 MiB of HBM per device.

```python
import jax
import jax.numpy as jnp
from jax import lax

W = 256
NT = 96
O = 384
NOCC = 32
NVIR = 1600
P_SIZE = 24576


def draw_integrals(key, part):
    base_key = jax.random.fold_in(key, 11)
    key_one = jax.random.fold_in(base_key, 0)
    sample = jax.random.normal(key_one, (NT * W, NT * W), jnp.float32)
    return (sample + sample.T) * 0.5 ** 0.5 * (NT * W) ** (-0.5)


def draw_tile_mask(key, part):
    base_key = jax.random.fold_in(key, 23)
    key_one, key_two = jax.random.split(base_key)
    levels = jax.random.randint(key_one, (NT,), 0, 4)
    random_ints = jax.random.randint(key_two, (NT, NT), 0, 8)
    symmetric = jnp.triu(random_ints) + jnp.triu(random_ints, 1).T
    positions = jnp.arange(NT)
    keep = (symmetric < 1 + levels[:, None] + levels[None, :]) | (positions[:, None] == positions[None, :])
    return keep.astype(jnp.int32)


def occ_pairs(key):
    base_key = jax.random.fold_in(key, 37)
    key_one, key_two, key_three = jax.random.split(base_key, 3)
    shuffle = jax.random.permutation(key_one, O).astype(jnp.int32)
    pair_count = O // 2
    first_occ = jax.random.randint(key_two, (pair_count,), 0, NOCC)
    second_occ = (first_occ + 1 + jax.random.randint(key_three, (pair_count,), 0, NOCC - 1)) % NOCC
    even_cols = shuffle[0::2]
    odd_cols = shuffle[1::2]
    zero_cols = jnp.zeros((O,), jnp.int32)
    partner = zero_cols.at[even_cols].set(odd_cols).at[odd_cols].set(even_cols)
    occ_first = zero_cols.at[even_cols].set(first_occ).at[odd_cols].set(second_occ)
    occ_second = zero_cols.at[even_cols].set(second_occ).at[odd_cols].set(first_occ)
    return (partner, jnp.stack([occ_first, occ_second]).astype(jnp.int32))


def draw_occ_index(key, part):
    return occ_pairs(key)[1]


def draw_partner(key, part):
    return occ_pairs(key)[0]


def plant(drawn, stream_key, smallest, top_value):
    dims = drawn.shape
    place = [jax.random.randint(jax.random.fold_in(stream_key, axis), (), 0, dims[axis]) for axis in range(len(dims))]
    drawn = drawn.at[tuple(place)].set(smallest)
    longest = dims.index(max(dims))
    place[longest] = (place[longest] + 1) % dims[longest]
    return drawn.at[tuple(place)].set(top_value)


def steps_of(rng, dims, shards, least, largest):
    level = 1.0
    for axis_at, shards_of in shards:
        steps = jax.random.uniform(jax.random.fold_in(jax.random.fold_in(rng, 6), axis_at), (shards_of,), jnp.float32, least / len(shards), largest / len(shards))
        level = level * jnp.repeat(jnp.exp(steps), dims[axis_at] // shards_of).reshape((-1,) + (1,) * (len(dims) - 1 - axis_at))
    return level


def bell_draw(stream_key, shape, scale, most, pieces=(), held_as=jnp.bfloat16):
    entries = jax.random.normal(stream_key, shape, jnp.float32) * scale
    if len(pieces) > 0:
        entries = steps_of(stream_key, shape, pieces, -0.22, 0.18) * entries
    return jnp.clip(entries, min=-most, max=most).astype(held_as)


def setup_inputs(seed: int = 0) -> dict:
    splits = jax.random.split(jax.random.key(seed), 11)
    integrals = draw_integrals(jax.random.fold_in(splits[10], 71), 0)
    tile_mask = draw_tile_mask(jax.random.fold_in(splits[10], 71), 0)
    amplitudes = bell_draw(splits[2], (P_SIZE, O), 0.5, 4.0, ((0, 256),), jnp.float32)
    other_first = bell_draw(splits[3], (P_SIZE, O), 1.0, 6.0, ((0, 256),), jnp.float32)
    other_second = bell_draw(splits[4], (P_SIZE, O), 1.0, 6.0, ((0, 256),), jnp.float32)
    vir_index = plant(jax.random.randint(splits[5], (2, P_SIZE), 0, NVIR), jax.random.fold_in(splits[5], 1), 0, NVIR - 1).astype(jnp.int32)
    occ_index = draw_occ_index(jax.random.fold_in(splits[10], 71), 0)
    partner = draw_partner(jax.random.fold_in(splits[10], 71), 0)
    eps_vir = jnp.clip(jax.random.uniform(splits[8], (NVIR,), jnp.float32, 0.2, 3.0), 0.2, 3.0)
    eps_occ = jnp.clip(jax.random.uniform(splits[9], (NOCC,), jnp.float32, -2.0, -0.2), -2.0, -0.2)
    return {"integrals": integrals, "tile_mask": tile_mask, "amplitudes": amplitudes, "other_first": other_first, "other_second": other_second, "vir_index": vir_index, "occ_index": occ_index, "partner": partner, "eps_vir": eps_vir, "eps_occ": eps_occ}


precise = lax.Precision.HIGHEST


def ladder_sum(integrals, tile_mask, amplitude):
    def one_tile_row(tile_row):
        rows_part = lax.dynamic_slice_in_dim(integrals, tile_row * W, W, 0)
        weights = jnp.repeat(tile_mask[tile_row].astype(jnp.float32), W)
        return jnp.dot(rows_part * weights[None, :], amplitude, precision=precise, preferred_element_type=jnp.float32)

    stacked = lax.map(one_tile_row, jnp.arange(NT, dtype=jnp.int32))
    return stacked.reshape(NT * W, amplitude.shape[1])


def renew(ladder, other, denominator, partner):
    unscaled = (other + ladder) / denominator
    return 0.5 * (unscaled - jnp.take(unscaled, partner, axis=1))


def reference(integrals, tile_mask, amplitudes, other_first, other_second, vir_index, occ_index, partner, eps_vir, eps_occ):
    vir_energy = eps_vir[vir_index[0]] + eps_vir[vir_index[1]]
    occ_energy = eps_occ[occ_index[0]] + eps_occ[occ_index[1]]
    denominator = vir_energy[:, None] - occ_energy[None, :]
    first_update = renew(ladder_sum(integrals, tile_mask, amplitudes), other_first, denominator, partner)
    second_update = renew(ladder_sum(integrals, tile_mask, first_update), other_second, denominator, partner)
    return first_update, second_update
```

```python
import jax
import jax.numpy as jnp
from jax import lax
from jax.sharding import PartitionSpec as P

W = 256

exact = lax.Precision.HIGHEST
three = lax.Precision.HIGH


def pick(index, table):
    places = lax.broadcasted_iota(jnp.int32, (index.shape[0], table.shape[0]), 1)
    hits = (index[:, None] == places).astype(jnp.float32)
    return jnp.sum(hits * table[None, :], axis=1)


def pair_energy(pair_index, table):
    return pick(pair_index[0], table) + pick(pair_index[1], table)


def pair_map(partner):
    cols = partner.shape[0]
    here = lax.broadcasted_iota(jnp.int32, (cols,), 0)
    first = here < partner
    key = jnp.minimum(here, partner)
    couple = jnp.sum((first[None, :] & (here[None, :] < key[:, None])).astype(jnp.int32), axis=1)
    hit = couple[:, None] == lax.broadcasted_iota(jnp.int32, (cols, cols // 2), 1)
    return jnp.where(hit, jnp.where(first, 1.0, -1.0)[:, None], 0.0)


def per_device(
    integrals,
    tile_mask,
    amplitudes,
    other_first,
    other_second,
    vir_index,
    occ_index,
    partner,
    eps_vir,
    eps_occ,
):
    row_count, col_count = integrals.shape
    tiles_down, tiles_across = tile_mask.shape
    weights = tile_mask.astype(jnp.float32)
    screened = (
        integrals.reshape(tiles_down, W, tiles_across, W) * weights[:, None, :, None]
    ).reshape(row_count, col_count)
    pairs = pair_map(partner)
    occ_energy = pair_energy(occ_index, eps_occ)
    occ_energy = jnp.sum(jnp.where(pairs > 0, occ_energy[:, None], 0.0), axis=0)
    n_con = lax.axis_size("con")
    n_res = lax.axis_size("res")
    con_at = lax.axis_index("con")
    res_at = lax.axis_index("res")
    fine_rows = amplitudes.shape[0]

    def differences(block):
        return jnp.dot(block, pairs, precision=exact, preferred_element_type=jnp.float32)

    def spread(half):
        return 0.5 * lax.dot_general(
            half, pairs, (((1,), (1,)), ((), ())), precision=exact, preferred_element_type=jnp.float32
        )

    def denominator(offset):
        picked = lax.dynamic_slice_in_dim(vir_index, offset, fine_rows, 1)
        return pair_energy(picked, eps_vir)[:, None] - occ_energy[None, :]

    own = differences(amplitudes)
    partial_one = jnp.dot(
        screened,
        lax.all_gather(own, "res", axis=0, tiled=True),
        precision=three,
        preferred_element_type=jnp.float32,
    )
    ladder_one = lax.psum_scatter(partial_one, "con", scatter_dimension=0, tiled=True)
    first = (differences(other_first) + ladder_one) / denominator((res_at * n_con + con_at) * fine_rows)
    partial_two = lax.dot_general(
        screened,
        lax.all_gather(first, "con", axis=0, tiled=True),
        (((0,), (0,)), ((), ())),
        precision=three,
        preferred_element_type=jnp.float32,
    )
    ladder_two = lax.psum_scatter(partial_two, "res", scatter_dimension=0, tiled=True)
    second = (differences(other_second) + ladder_two) / denominator((con_at * n_res + res_at) * fine_rows)
    return (spread(first), spread(second))


def solution(mesh):
    return jax.shard_map(
        per_device,
        mesh=mesh,
        in_specs=(
            P("res", "con"),
            P("res", "con"),
            P(("con", "res"), None),
            P(("res", "con"), None),
            P(("con", "res"), None),
            P(),
            P(),
            P(),
            P(),
            P(),
        ),
        out_specs=(P(("res", "con"), None), P(("con", "res"), None)),
        check_vma=False,
    )
```

```python
import jax
import jax.numpy as jnp
from jax import lax
from jax.experimental import pallas as pl
from jax.experimental.pallas import tpu as pltpu
from jax.sharding import PartitionSpec as P

W = 256
MESH = pl.DeviceIdType.MESH
exact = lax.Precision.HIGHEST

N_X, N_C, N_H, N_Y, N_L = 4, 2, 2, 4, 4
CHUNKS = ((0, 96, 128), (96, 48, 64))
N_SEMS = 96


def pick(index, table):
    places = lax.broadcasted_iota(jnp.int32, (index.shape[0], table.shape[0]), 1)
    hits = (index[:, None] == places).astype(jnp.float32)
    return jnp.sum(hits * table[None, :], axis=1)


def pair_energy(pair_index, table):
    return pick(pair_index[0], table) + pick(pair_index[1], table)


def pair_map(partner):
    cols = partner.shape[0]
    here = lax.broadcasted_iota(jnp.int32, (cols,), 0)
    first = here < partner
    key = jnp.minimum(here, partner)
    couple = jnp.sum((first[None, :] & (here[None, :] < key[:, None])).astype(jnp.int32), axis=1)
    hit = couple[:, None] == lax.broadcasted_iota(jnp.int32, (cols, cols // 2), 1)
    return jnp.where(hit, jnp.where(first, 1.0, -1.0)[:, None], 0.0)


def pack(block):
    low = jnp.concatenate([block[:48, 128:], block[48:, 128:]], axis=1)
    return jnp.concatenate([block[:, :128], low], axis=0)


def unpack(block):
    low = block[96:]
    return jnp.concatenate([block[:96], jnp.concatenate([low[:, :64], low[:, 64:]], axis=0)], axis=1)


def ladder_kernel(
    integrals, mask, own, oth1, oth2, den1, den2, out1, out2, stage, hi, lo, hi_t, lo_t, cat_a, cat_b, oth1_peer, *rest
):
    n = len(CHUNKS)
    per = 12
    bufs = [rest[per * k : per * k + per] for k in range(n)]
    stage_sem, ssem, rsem = rest[per * n :]
    con = lax.axis_index("con")
    res = lax.axis_index("res")
    zh, x, c = con // 8, (con // 2) % 4, con % 2
    y, zl = res // 4, res % 4
    cats = (cat_a, cat_b)

    def wrap(v, m):
        return lax.rem(v + m, m)

    def at(zh_=None, x_=None, c_=None, y_=None, zl_=None):
        zh_ = zh if zh_ is None else zh_
        x_ = x if x_ is None else x_
        c_ = c if c_ is None else c_
        y_ = y if y_ is None else y_
        zl_ = zl if zl_ is None else zl_
        return (zh_ * 8 + x_ * 2 + c_, y_ * 4 + zl_)

    used = [0]
    sent = []

    def take(count):
        first = used[0]
        used[0] += count
        return first

    def describe(index, src, dst, device):
        return pltpu.make_async_remote_copy(
            src_ref=src, dst_ref=dst, send_sem=ssem.at[index], recv_sem=rsem.at[index],
            device_id=device, device_id_type=MESH,
        )

    def send(src, dst, device):
        copy = describe(take(1), src, dst, device)
        copy.start()
        sent.append(copy)
        return copy

    loads = [
        pltpu.make_async_copy(integrals.at[pl.ds(i * W, W)], stage.at[i], stage_sem.at[i]) for i in range(6)
    ]
    for load in loads:
        load.start()

    peers = (
        [at(zl_=wrap(zl + d, 4)) for d in (1, 2, 3)]
        + [at(y_=wrap(y + d, 4)) for d in (1, 2, 3)]
        + [at(x_=wrap(x + d, 4)) for d in (1, 2, 3)]
        + [at(c_=1 - c), at(zh_=1 - zh)]
    )
    barrier = pltpu.get_barrier_semaphore()
    for peer in peers:
        pl.semaphore_signal(barrier, inc=1, device_id=peer, device_id_type=MESH)
    pl.semaphore_wait(barrier, len(peers))

    gather_z = [None] * n
    gather_y = [[] for _ in range(n)]

    def spread_y(k, j, src):
        gat = bufs[k][0]
        slot = wrap(zl - j + 4, 4)
        for d in (1, 2, 3):
            gather_y[k].append(send(src, gat.at[y, slot], at(y_=wrap(y + d, 4))))

    def start_gather(k):
        row, rows, _ = CHUNKS[k]
        gat = bufs[k][0]
        mine = own.at[pl.ds(row, rows)]
        gather_z[k] = [send(mine, gat.at[y, zl], at(zl_=wrap(zl + d, 4))) for d in (1, 2, 3)]
        spread_y(k, 0, mine)
        gat[y, zl] = own[row : row + rows]

    def forward(k, j):
        gat = bufs[k][0]
        gather_z[k][j - 1].wait_recv()
        spread_y(k, j, gat.at[y, wrap(zl - j + 4, 4)])

    def split_tile(i):
        loads[i].wait()

        def body(j, carry):
            cols = pl.ds(pl.multiple_of(j * W, W), W)
            v = stage[i, :, cols] * mask[i, j].astype(jnp.float32)
            h = v.astype(jnp.bfloat16)
            hi[i * W : (i + 1) * W, cols] = h
            lo[i * W : (i + 1) * W, cols] = (v - h.astype(jnp.float32)).astype(jnp.bfloat16)
            return carry

        lax.fori_loop(0, 6, body, 0)

    def turn(first, last):
        def body(t, carry):
            rows = pl.ds(pl.multiple_of((t // 6) * W, W), W)
            cols = pl.ds(pl.multiple_of((t % 6) * W, W), W)
            hi_t[cols, rows] = hi[rows, cols].T
            lo_t[cols, rows] = lo[rows, cols].T
            return carry

        lax.fori_loop(first, last, body, 0)

    def fill_cat(k, b, slab):
        width = CHUNKS[k][2]
        cat = cats[k]
        high = slab.astype(jnp.bfloat16).astype(jnp.float32)
        low = slab - high
        if width == 128:
            cat[96 * b : 96 * b + 96, 0:128] = high.astype(jnp.bfloat16)
            cat[96 * b : 96 * b + 96, 128:256] = low.astype(jnp.bfloat16)
        else:
            left = lax.broadcasted_iota(jnp.int32, slab.shape, 1) < 64
            top = jnp.where(left, high, pltpu.roll(low, 64, 1))
            bottom = jnp.where(left, pltpu.roll(high, 64, 1), low)
            cat[96 * b : 96 * b + 48, :] = top.astype(jnp.bfloat16)
            cat[96 * b + 48 : 96 * b + 96, :] = bottom.astype(jnp.bfloat16)

    def quarter(k, high, low, it):
        width = CHUNKS[k][2]
        cat = cats[k]
        rows = pl.ds(pl.multiple_of(it * 384, 384), 384)
        total = jnp.dot(high[rows, :], cat[...], preferred_element_type=jnp.float32)
        total = total + jnp.dot(low[rows, :], cat[...], preferred_element_type=jnp.float32)
        if width == 128:
            total = total[:, :128] + total[:, 128:]
            return [total[96 * p : 96 * p + 96] for p in range(4)]
        total = total + pltpu.roll(total, 64, 1)
        left = lax.broadcasted_iota(jnp.int32, (48, 128), 1) < 64
        return [
            jnp.where(left, total[96 * p : 96 * p + 48], total[96 * p + 48 : 96 * p + 96]) for p in range(4)
        ]

    core_copies = [None] * n

    def first_product(k):
        gat, par, corr = bufs[k][0], bufs[k][1], bufs[k][2]
        for copy in gather_y[k]:
            copy.wait_recv()
        for b in range(16):
            fill_cat(k, b, gat[b // 4, b % 4])
        base = take(4)

        def core_copy(it):
            h, xs = it // 2, pl.ds(2 * (it % 2), 2)
            return describe(base + it, par.at[1 - c, h, xs], corr.at[h, xs], at(c_=1 - c))

        def body(it, carry):
            slabs = quarter(k, hi, lo, it)
            for p in range(4):
                par[p % 2, it // 2, 2 * (it % 2) + p // 2] = slabs[p]
            core_copy(it).start()
            return carry

        lax.fori_loop(0, 4, body, 0)
        core_copies[k] = [core_copy(it) for it in range(4)]
        sent.extend(core_copies[k])

    x_copies = [None] * n

    def reduce_x(k):
        par, corr, xsum, xrecv = bufs[k][1], bufs[k][2], bufs[k][3], bufs[k][4]
        for copy in core_copies[k]:
            copy.wait_recv()
        x_copies[k] = []
        for d in (2, 1, 3, 0):
            xd = wrap(x + d, 4)
            for h in range(2):
                xsum[xd, h] = par[c, h, xd] + corr[h, xd]
            if d:
                x_copies[k].append(send(xsum.at[xd], xrecv.at[d - 1], at(x_=xd)))

    h_copies = [None] * n

    def reduce_h(k):
        xsum, xrecv, hsum, hrecv = bufs[k][3], bufs[k][4], bufs[k][5], bufs[k][6]
        for copy in x_copies[k]:
            copy.wait_recv()
        for h in range(2):
            hsum[h] = (xsum[x, h] + xrecv[1, h]) + (xrecv[0, h] + xrecv[2, h])
        h_copies[k] = send(hsum, hrecv, at(zh_=1 - zh))

    ux_copies = [None] * n
    uc_copies = [None] * n

    def forward_core(k, xd):
        ug = bufs[k][7]
        uc_copies[k].append(send(ug.at[c, xd], ug.at[c, xd], at(c_=1 - c)))

    def update_one(k):
        row, rows, _ = CHUNKS[k]
        hsum, hrecv, ug = bufs[k][5], bufs[k][6], bufs[k][7]
        h_copies[k].wait_recv()
        here = slice(row, row + rows)
        both = []
        for h in range(2):
            other = jnp.where(zh == h, oth1[here, :], oth1_peer[here, :])
            value = (other + (hsum[h] + hrecv[h])) / den1[h, here, :]
            ug[c, x, h] = value
            both.append(value)
        ux_copies[k] = []
        uc_copies[k] = []
        for d in (2, 1, 3):
            ux_copies[k].append(send(ug.at[c, x], ug.at[c, x], at(x_=wrap(x + d, 4))))
        forward_core(k, x)
        out1[here, :] = jnp.where(zh == 0, both[0], both[1])

    def pass_core(k):
        for copy, d in zip(ux_copies[k], (2, 1, 3)):
            copy.wait_recv()
            forward_core(k, wrap(x - d + 4, 4))

    y_copies = [None] * n

    def second_product(k):
        ug, par, yrecv = bufs[k][7], bufs[k][8], bufs[k][9]
        for copy in uc_copies[k]:
            copy.wait_recv()
        for b in range(16):
            fill_cat(k, b, ug[b % 2, (b // 2) % 4, b // 8])
        base = take(3)

        def y_copy(it):
            yd = wrap(y + 1 + it, 4)
            return describe(base + it, par.at[yd], yrecv.at[it], at(y_=yd))

        def body(it, carry):
            yd = wrap(y + 1 + it, 4)
            slabs = quarter(k, hi_t, lo_t, yd)
            for p in range(4):
                par[yd, p] = slabs[p]

            @pl.when(it < 3)
            def _():
                y_copy(it).start()

            return carry

        lax.fori_loop(0, 4, body, 0)
        y_copies[k] = [y_copy(it) for it in range(3)]
        sent.extend(y_copies[k])

    l_copies = [None] * n

    def reduce_l(k):
        par, yrecv, ysum, lrecv = bufs[k][8], bufs[k][9], bufs[k][10], bufs[k][11]
        for copy in y_copies[k]:
            copy.wait_recv()
        l_copies[k] = []
        for d in (2, 1, 3, 0):
            ld = wrap(zl + d, 4)
            ysum[ld] = (par[y, ld] + yrecv[0, ld]) + (yrecv[1, ld] + yrecv[2, ld])
            if d:
                l_copies[k].append(send(ysum.at[ld], lrecv.at[d - 1], at(zl_=ld)))

    def update_two(k):
        row, rows, _ = CHUNKS[k]
        ysum, lrecv = bufs[k][10], bufs[k][11]
        for copy in l_copies[k]:
            copy.wait_recv()
        here = slice(row, row + rows)
        ladder = (ysum[zl] + lrecv[0]) + (lrecv[1] + lrecv[2])
        out2[here, :] = (oth2[here, :] + ladder) / den2[here, :]

    start_gather(0)
    start_gather(1)
    other_copy = send(oth1, oth1_peer, at(zh_=1 - zh))
    split_tile(0)
    split_tile(1)
    for j in (1, 3, 2):
        forward(0, j)
    split_tile(2)
    for j in (1, 3, 2):
        forward(1, j)
    for i in (3, 4, 5):
        split_tile(i)
    first_product(0)
    turn(0, 12)
    reduce_x(0)
    first_product(1)
    turn(12, 24)
    reduce_h(0)
    reduce_x(1)
    turn(24, 36)
    other_copy.wait_recv()
    update_one(0)
    reduce_h(1)
    pass_core(0)
    update_one(1)
    second_product(0)
    pass_core(1)
    second_product(1)
    reduce_l(0)
    update_two(0)
    reduce_l(1)
    update_two(1)
    for copy in sent:
        copy.wait_send()


def run_ladders(integrals, tile_mask, own, oth1, oth2, den1, den2):
    f32, bf16 = jnp.float32, jnp.bfloat16
    side = integrals.shape[0]
    scratch = [
        pltpu.VMEM((6, W, side), f32),
        pltpu.VMEM((side, side), bf16),
        pltpu.VMEM((side, side), bf16),
        pltpu.VMEM((side, side), bf16),
        pltpu.VMEM((side, side), bf16),
        pltpu.VMEM((side, 256), bf16),
        pltpu.VMEM((side, 128), bf16),
        pltpu.VMEM(own.shape, f32),
    ]
    for _, rows, _ in CHUNKS:
        for lead in (
            (4, 4), (2, 2, 4), (2, 4), (4, 2), (3, 2), (2,), (2,), (2, 4, 2), (4, 4), (3, 4), (4,), (3,)
        ):
            scratch.append(pltpu.VMEM(lead + (rows, 128), f32))
    scratch += [
        pltpu.SemaphoreType.DMA((6,)),
        pltpu.SemaphoreType.DMA((N_SEMS,)),
        pltpu.SemaphoreType.DMA((N_SEMS,)),
    ]
    vmem = pl.BlockSpec(memory_space=pltpu.VMEM)
    return pl.pallas_call(
        ladder_kernel,
        out_shape=[jax.ShapeDtypeStruct(own.shape, f32)] * 2,
        in_specs=[pl.BlockSpec(memory_space=pl.ANY), pl.BlockSpec(memory_space=pltpu.SMEM)] + [vmem] * 5,
        out_specs=[vmem, vmem],
        scratch_shapes=scratch,
        compiler_params=pltpu.CompilerParams(
            collective_id=0, has_side_effects=True, vmem_limit_bytes=56 * 1024 * 1024
        ),
        name="ladders",
    )(integrals, tile_mask, own, oth1, oth2, den1, den2)


def per_device(
    integrals,
    tile_mask,
    amplitudes,
    other_first,
    other_second,
    vir_index,
    occ_index,
    partner,
    eps_vir,
    eps_occ,
):
    pairs = pair_map(partner)
    occ_energy = pair_energy(occ_index, eps_occ)
    occ_energy = jnp.sum(jnp.where(pairs > 0, occ_energy[:, None], 0.0), axis=0)
    con_at = lax.axis_index("con")
    res_at = lax.axis_index("res")
    fine_rows = amplitudes.shape[0]

    def differences(block):
        return pack(jnp.dot(block, pairs, precision=exact, preferred_element_type=jnp.float32))

    def spread(half):
        return 0.5 * lax.dot_general(
            unpack(half), pairs, (((1,), (1,)), ((), ())), precision=exact, preferred_element_type=jnp.float32
        )

    def denominator(block):
        picked = lax.dynamic_slice_in_dim(vir_index, block * fine_rows, fine_rows, 1)
        return pack(pair_energy(picked, eps_vir)[:, None] - occ_energy[None, :])

    den1 = jnp.stack([denominator(res_at * 16 + h * 8 + con_at % 8) for h in range(2)])
    den2 = denominator(con_at * 16 + res_at)
    first, second = run_ladders(
        integrals,
        tile_mask,
        differences(amplitudes),
        differences(other_first),
        differences(other_second),
        den1,
        den2,
    )
    return (spread(first), spread(second))


def solution(mesh):
    return jax.shard_map(
        per_device,
        mesh=mesh,
        in_specs=(
            P("res", "con"),
            P("res", "con"),
            P(("con", "res"), None),
            P(("res", "con"), None),
            P(("con", "res"), None),
            P(),
            P(),
            P(),
            P(),
            P(),
        ),
        out_specs=(P(("res", "con"), None), P(("con", "res"), None)),
        check_vma=False,
    )
```

```python
import jax
import jax.numpy as jnp
from jax import lax
from jax.experimental import pallas as pl
from jax.experimental.pallas import tpu as pltpu
from jax.sharding import PartitionSpec as P

W = 256
MESH = pl.DeviceIdType.MESH

N_X, N_C, N_H, N_Y, N_L = 4, 2, 2, 4, 4
CHUNKS = ((0, 48, 64), (48, 48, 64), (96, 48, 64))
N_SEMS = 128


def split_three(v):
    one = v.astype(jnp.bfloat16)
    v = v - one.astype(jnp.float32)
    two = v.astype(jnp.bfloat16)
    three = (v - two.astype(jnp.float32)).astype(jnp.bfloat16)
    return jnp.concatenate([one, two, three], axis=0)


def join_three(v):
    n = v.shape[0] // 3
    return (v[2 * n :] + v[n : 2 * n]) + v[:n]


def ladder_kernel(
    integrals, mask, amplitudes, other_first, other_second, vir_index, occ_index, partner, eps_vir, eps_occ,
    out1, out2, stage, hi, lo, hi_t, lo_t, cat_a, cat_b, cat_c, own, oth1, oth1_peer, oth2, den1, den2, new1, new2,
    pairs, window, *rest
):
    n = len(CHUNKS)
    per = 12
    bufs = [rest[per * k : per * k + per] for k in range(n)]
    stage_sem, window_sem, ssem, rsem = rest[per * n :]
    con = lax.axis_index("con")
    res = lax.axis_index("res")
    zh, x, c = con // 8, (con // 2) % 4, con % 2
    y, zl = res // 4, res % 4
    cats = (cat_a, cat_b, cat_c)

    def wrap(v, m):
        return lax.rem(v + m, m)

    def at(zh_=None, x_=None, c_=None, y_=None, zl_=None):
        zh_ = zh if zh_ is None else zh_
        x_ = x if x_ is None else x_
        c_ = c if c_ is None else c_
        y_ = y if y_ is None else y_
        zl_ = zl if zl_ is None else zl_
        return (zh_ * 8 + x_ * 2 + c_, y_ * 4 + zl_)

    used = [0]
    sent = []

    def take(count):
        first = used[0]
        used[0] += count
        return first

    def describe(index, src, dst, device):
        return pltpu.make_async_remote_copy(
            src_ref=src, dst_ref=dst, send_sem=ssem.at[index], recv_sem=rsem.at[index],
            device_id=device, device_id_type=MESH,
        )

    def send(src, dst, device):
        copy = describe(take(1), src, dst, device)
        copy.start()
        sent.append(copy)
        return copy

    loads = [
        pltpu.make_async_copy(integrals.at[pl.ds(i * W, W)], stage.at[i], stage_sem.at[i]) for i in range(6)
    ]
    for load in loads:
        load.start()

    blocks = (res * 16 + con % 8, res * 16 + 8 + con % 8, con * 16 + res)
    shifts, windows = [], []
    for i, block in enumerate(blocks):
        first = lax.min(block * 96 // 128 * 128, vir_index.shape[1] - 256)
        first = pl.multiple_of(first, 128)
        shifts.append(block * 96 - first)
        windows.append(
            pltpu.make_async_copy(vir_index.at[:, pl.ds(first, 256)], window.at[i], window_sem.at[i])
        )
        windows[i].start()

    peers = (
        [at(zl_=wrap(zl + d, 4)) for d in (1, 2, 3)]
        + [at(y_=wrap(y + d, 4)) for d in (1, 2, 3)]
        + [at(x_=wrap(x + d, 4)) for d in (1, 2, 3)]
        + [at(c_=1 - c), at(zh_=1 - zh)]
    )
    barrier = pltpu.get_barrier_semaphore()
    for peer in peers:
        pl.semaphore_signal(barrier, inc=1, device_id=peer, device_id_type=MESH)
    half = lax.broadcasted_iota(jnp.int32, (48, 128), 1) < 64

    def map_pairs():
        size = partner.shape[1]
        row = partner[...].astype(jnp.float32)
        col = jnp.broadcast_to(row, (128, size)).T
        col = jnp.concatenate([col] * (size // 128), axis=1)
        down = lax.broadcasted_iota(jnp.int32, (size, size), 0).astype(jnp.float32)
        across = lax.broadcasted_iota(jnp.int32, (size, size), 1)
        wide = across.astype(jnp.float32)
        before = (wide < jnp.minimum(down, col)) & (wide < jnp.broadcast_to(row, (size, size)))
        before = jnp.where(before, 1.0, 0.0).astype(jnp.bfloat16)
        couple = jnp.dot(before, jnp.ones((size, size), jnp.bfloat16), preferred_element_type=jnp.float32)
        place = (64 * (across // 128) + across % 64).astype(jnp.float32)
        sign = jnp.where(down < col, 1.0, -1.0)
        pairs[...] = jnp.where(couple == place, sign, 0.0).astype(jnp.bfloat16)

    def differences(src, dst):
        wide = join_three(jnp.dot(split_three(src[...]), pairs[...], preferred_element_type=jnp.float32))
        for k in range(n):
            part = wide[:, 128 * k : 128 * k + 128]
            dst[48 * k : 48 * k + 48, :] = jnp.where(half, part[:48], part[48:])

    def expand(src, dst):
        parts = [src[48 * k : 48 * k + 48, :] for k in range(n)]
        top = jnp.concatenate([jnp.where(half, part, 0.0) for part in parts], axis=1)
        bottom = jnp.concatenate([jnp.where(half, 0.0, part) for part in parts], axis=1)
        both = split_three(0.5 * jnp.concatenate([top, bottom], axis=0))
        dst[...] = join_three(
            lax.dot_general(both, pairs[...], (((1,), (1,)), ((), ())), preferred_element_type=jnp.float32)
        )

    def denominators():
        occ = occ_index[...]
        picked = jnp.zeros(occ.shape, jnp.float32)
        for i in range(eps_occ.shape[0]):
            picked = jnp.where(occ == i, eps_occ[i], picked)
        energy = jnp.broadcast_to(picked[0:1] + picked[1:2], (16, occ.shape[1]))
        firsts = jnp.maximum(pairs[...].astype(jnp.float32), 0.0).astype(jnp.bfloat16)
        occ_row = join_three(jnp.dot(split_three(energy), firsts, preferred_element_type=jnp.float32))[0:1]
        table = split_three(jnp.broadcast_to(eps_vir[...], (16, eps_vir.shape[1])))
        orbitals = lax.broadcasted_iota(jnp.int32, (eps_vir.shape[1], 256), 0)
        for i in range(3):
            windows[i].wait()
            found = window[i]
            counts = jnp.where(orbitals == found[0:1], 1.0, 0.0) + jnp.where(orbitals == found[1:2], 1.0, 0.0)
            vir = join_three(jnp.dot(table, counts.astype(jnp.bfloat16), preferred_element_type=jnp.float32))
            vir = pltpu.roll(vir, lax.rem(256 - shifts[i], 256), 1)[0:1, 0:128]
            vir = jnp.broadcast_to(vir, (128, 128)).T
            vir = jnp.where(half, vir[:48], vir[48:96])
            for k in range(n):
                value = vir - occ_row[:, 128 * k : 128 * k + 128]
                if i < 2:
                    den1[i, 48 * k : 48 * k + 48, :] = value
                else:
                    den2[48 * k : 48 * k + 48, :] = value

    map_pairs()
    differences(amplitudes, own)
    pl.semaphore_wait(barrier, len(peers))

    gather_z = [None] * n
    gather_y = [[] for _ in range(n)]

    def spread_y(k, j, src):
        gat = bufs[k][0]
        slot = wrap(zl - j + 4, 4)
        for d in (1, 2, 3):
            gather_y[k].append(send(src, gat.at[y, slot], at(y_=wrap(y + d, 4))))

    def start_gather(k):
        row, rows, _ = CHUNKS[k]
        gat = bufs[k][0]
        mine = own.at[pl.ds(row, rows)]
        gather_z[k] = [send(mine, gat.at[y, zl], at(zl_=wrap(zl + d, 4))) for d in (1, 2, 3)]
        spread_y(k, 0, mine)
        gat[y, zl] = own[row : row + rows]

    def forward(k, j):
        gat = bufs[k][0]
        gather_z[k][j - 1].wait_recv()
        spread_y(k, j, gat.at[y, wrap(zl - j + 4, 4)])

    def split_tile(i):
        loads[i].wait()

        def body(j, carry):
            cols = pl.ds(pl.multiple_of(j * W, W), W)
            v = stage[i, :, cols] * mask[i, j].astype(jnp.float32)
            h = v.astype(jnp.bfloat16)
            hi[i * W : (i + 1) * W, cols] = h
            lo[i * W : (i + 1) * W, cols] = (v - h.astype(jnp.float32)).astype(jnp.bfloat16)
            return carry

        lax.fori_loop(0, 6, body, 0)

    def turn(first, last):
        def body(t, carry):
            rows = pl.ds(pl.multiple_of((t // 6) * W, W), W)
            cols = pl.ds(pl.multiple_of((t % 6) * W, W), W)
            hi_t[cols, rows] = hi[rows, cols].T
            lo_t[cols, rows] = lo[rows, cols].T
            return carry

        lax.fori_loop(first, last, body, 0)

    def fill_cat(k, b, slab):
        width = CHUNKS[k][2]
        cat = cats[k]
        high = slab.astype(jnp.bfloat16).astype(jnp.float32)
        low = slab - high
        if width == 128:
            cat[96 * b : 96 * b + 96, 0:128] = high.astype(jnp.bfloat16)
            cat[96 * b : 96 * b + 96, 128:256] = low.astype(jnp.bfloat16)
        else:
            left = lax.broadcasted_iota(jnp.int32, slab.shape, 1) < 64
            top = jnp.where(left, high, pltpu.roll(low, 64, 1))
            bottom = jnp.where(left, pltpu.roll(high, 64, 1), low)
            cat[96 * b : 96 * b + 48, :] = top.astype(jnp.bfloat16)
            cat[96 * b + 48 : 96 * b + 96, :] = bottom.astype(jnp.bfloat16)

    def quarter(k, high, low, it):
        width = CHUNKS[k][2]
        cat = cats[k]
        rows = pl.ds(pl.multiple_of(it * 384, 384), 384)
        total = jnp.dot(high[rows, :], cat[...], preferred_element_type=jnp.float32)
        total = total + jnp.dot(low[rows, :], cat[...], preferred_element_type=jnp.float32)
        if width == 128:
            total = total[:, :128] + total[:, 128:]
            return [total[96 * p : 96 * p + 96] for p in range(4)]
        total = total + pltpu.roll(total, 64, 1)
        left = lax.broadcasted_iota(jnp.int32, (48, 128), 1) < 64
        return [
            jnp.where(left, total[96 * p : 96 * p + 48], total[96 * p + 48 : 96 * p + 96]) for p in range(4)
        ]

    core_copies = [None] * n

    def first_product(k):
        gat, par, corr = bufs[k][0], bufs[k][1], bufs[k][2]
        for copy in gather_y[k]:
            copy.wait_recv()
        for b in range(16):
            fill_cat(k, b, gat[b // 4, b % 4])
        base = take(4)

        def core_copy(it):
            h, xs = it // 2, pl.ds(2 * (it % 2), 2)
            return describe(base + it, par.at[1 - c, h, xs], corr.at[h, xs], at(c_=1 - c))

        def body(it, carry):
            slabs = quarter(k, hi, lo, it)
            for p in range(4):
                par[p % 2, it // 2, 2 * (it % 2) + p // 2] = slabs[p]
            core_copy(it).start()
            return carry

        lax.fori_loop(0, 4, body, 0)
        core_copies[k] = [core_copy(it) for it in range(4)]
        sent.extend(core_copies[k])

    x_copies = [None] * n

    def reduce_x(k):
        par, corr, xsum, xrecv = bufs[k][1], bufs[k][2], bufs[k][3], bufs[k][4]
        for copy in core_copies[k]:
            copy.wait_recv()
        x_copies[k] = []
        for d in (2, 1, 3, 0):
            xd = wrap(x + d, 4)
            for h in range(2):
                xsum[xd, h] = par[c, h, xd] + corr[h, xd]
            if d:
                x_copies[k].append(send(xsum.at[xd], xrecv.at[d - 1], at(x_=xd)))

    h_copies = [None] * n

    def reduce_h(k):
        xsum, xrecv, hsum, hrecv = bufs[k][3], bufs[k][4], bufs[k][5], bufs[k][6]
        for copy in x_copies[k]:
            copy.wait_recv()
        for h in range(2):
            hsum[h] = (xsum[x, h] + xrecv[1, h]) + (xrecv[0, h] + xrecv[2, h])
        h_copies[k] = send(hsum, hrecv, at(zh_=1 - zh))

    ux_copies = [None] * n
    uc_copies = [None] * n

    def forward_core(k, xd):
        ug = bufs[k][7]
        uc_copies[k].append(send(ug.at[c, xd], ug.at[c, xd], at(c_=1 - c)))

    def update_one(k):
        row, rows, _ = CHUNKS[k]
        hsum, hrecv, ug = bufs[k][5], bufs[k][6], bufs[k][7]
        h_copies[k].wait_recv()
        here = slice(row, row + rows)
        both = []
        for h in range(2):
            other = jnp.where(zh == h, oth1[here, :], oth1_peer[here, :])
            value = (other + (hsum[h] + hrecv[h])) / den1[h, here, :]
            ug[c, x, h] = value
            both.append(value)
        ux_copies[k] = []
        uc_copies[k] = []
        for d in (2, 1, 3):
            ux_copies[k].append(send(ug.at[c, x], ug.at[c, x], at(x_=wrap(x + d, 4))))
        forward_core(k, x)
        new1[here, :] = jnp.where(zh == 0, both[0], both[1])

    def pass_core(k):
        for copy, d in zip(ux_copies[k], (2, 1, 3)):
            copy.wait_recv()
            forward_core(k, wrap(x - d + 4, 4))

    y_copies = [None] * n

    def second_product(k):
        ug, par, yrecv = bufs[k][7], bufs[k][8], bufs[k][9]
        for copy in uc_copies[k]:
            copy.wait_recv()
        for b in range(16):
            fill_cat(k, b, ug[b % 2, (b // 2) % 4, b // 8])
        base = take(3)

        def y_copy(it):
            yd = wrap(y + 1 + it, 4)
            return describe(base + it, par.at[yd], yrecv.at[it], at(y_=yd))

        def body(it, carry):
            yd = wrap(y + 1 + it, 4)
            slabs = quarter(k, hi_t, lo_t, yd)
            for p in range(4):
                par[yd, p] = slabs[p]

            @pl.when(it < 3)
            def _():
                y_copy(it).start()

            return carry

        lax.fori_loop(0, 4, body, 0)
        y_copies[k] = [y_copy(it) for it in range(3)]
        sent.extend(y_copies[k])

    l_copies = [None] * n

    def reduce_l(k):
        par, yrecv, ysum, lrecv = bufs[k][8], bufs[k][9], bufs[k][10], bufs[k][11]
        for copy in y_copies[k]:
            copy.wait_recv()
        l_copies[k] = []
        for d in (2, 1, 3, 0):
            ld = wrap(zl + d, 4)
            ysum[ld] = (par[y, ld] + yrecv[0, ld]) + (yrecv[1, ld] + yrecv[2, ld])
            if d:
                l_copies[k].append(send(ysum.at[ld], lrecv.at[d - 1], at(zl_=ld)))

    def update_two(k):
        row, rows, _ = CHUNKS[k]
        ysum, lrecv = bufs[k][10], bufs[k][11]
        for copy in l_copies[k]:
            copy.wait_recv()
        here = slice(row, row + rows)
        ladder = (ysum[zl] + lrecv[0]) + (lrecv[1] + lrecv[2])
        new2[here, :] = (oth2[here, :] + ladder) / den2[here, :]

    start_gather(0)
    start_gather(1)
    start_gather(2)
    differences(other_first, oth1)
    other_copy = send(oth1, oth1_peer, at(zh_=1 - zh))
    split_tile(0)
    split_tile(1)
    forward(0, 1)
    forward(0, 3)
    forward(0, 2)
    split_tile(2)
    split_tile(3)
    forward(1, 1)
    forward(1, 3)
    forward(1, 2)
    split_tile(4)
    split_tile(5)
    forward(2, 1)
    forward(2, 3)
    forward(2, 2)
    denominators()
    first_product(0)
    turn(0, 12)
    reduce_x(0)
    first_product(1)
    reduce_h(0)
    reduce_x(1)
    first_product(2)
    other_copy.wait_recv()
    update_one(0)
    reduce_h(1)
    reduce_x(2)
    turn(12, 36)
    pass_core(0)
    update_one(1)
    reduce_h(2)
    second_product(0)
    pass_core(1)
    update_one(2)
    second_product(1)
    pass_core(2)
    reduce_l(0)
    second_product(2)
    differences(other_second, oth2)
    expand(new1, out1)
    reduce_l(1)
    update_two(0)
    reduce_l(2)
    update_two(1)
    update_two(2)
    expand(new2, out2)
    for copy in sent:
        copy.wait_send()


def per_device(
    integrals,
    tile_mask,
    amplitudes,
    other_first,
    other_second,
    vir_index,
    occ_index,
    partner,
    eps_vir,
    eps_occ,
):
    f32, bf16 = jnp.float32, jnp.bfloat16
    side = integrals.shape[0]
    packed = (144, 128)
    scratch = [pltpu.VMEM((6, W, side), f32)]
    scratch += [pltpu.VMEM((side, side), bf16)] * 4
    scratch += [pltpu.VMEM((side, 128), bf16)] * 3
    scratch += [pltpu.VMEM(packed, f32)] * 4
    scratch += [pltpu.VMEM((2,) + packed, f32)]
    scratch += [pltpu.VMEM(packed, f32)] * 3
    scratch += [pltpu.VMEM((384, 384), bf16), pltpu.VMEM((3, 2, 256), jnp.int32)]
    for _, rows, _ in CHUNKS:
        for lead in (
            (4, 4), (2, 2, 4), (2, 4), (4, 2), (3, 2), (2,), (2,), (2, 4, 2), (4, 4), (3, 4), (4,), (3,)
        ):
            scratch.append(pltpu.VMEM(lead + (rows, 128), f32))
    scratch += [
        pltpu.SemaphoreType.DMA((6,)),
        pltpu.SemaphoreType.DMA((3,)),
        pltpu.SemaphoreType.DMA((N_SEMS,)),
        pltpu.SemaphoreType.DMA((N_SEMS,)),
    ]
    vmem = pl.BlockSpec(memory_space=pltpu.VMEM)
    smem = pl.BlockSpec(memory_space=pltpu.SMEM)
    hbm = pl.BlockSpec(memory_space=pl.ANY)
    return pl.pallas_call(
        ladder_kernel,
        out_shape=[jax.ShapeDtypeStruct(amplitudes.shape, f32)] * 2,
        in_specs=[hbm, smem, vmem, vmem, vmem, hbm, vmem, vmem, vmem, smem],
        out_specs=[vmem, vmem],
        scratch_shapes=scratch,
        compiler_params=pltpu.CompilerParams(
            collective_id=0, has_side_effects=True, vmem_limit_bytes=56 * 1024 * 1024
        ),
        name="ladders",
    )(
        integrals, tile_mask, amplitudes, other_first, other_second, vir_index, occ_index,
        partner.reshape(1, -1), eps_vir.reshape(1, -1), eps_occ,
    )


def solution(mesh):
    return jax.shard_map(
        per_device,
        mesh=mesh,
        in_specs=(
            P("res", "con"),
            P("res", "con"),
            P(("con", "res"), None),
            P(("res", "con"), None),
            P(("con", "res"), None),
            P(),
            P(),
            P(),
            P(),
            P(),
        ),
        out_specs=(P(("res", "con"), None), P(("con", "res"), None)),
        check_vma=False,
    )
```

```python
import jax
import jax.numpy as jnp
from jax import lax
from jax.experimental import pallas as pl
from jax.experimental.pallas import tpu as pltpu
from jax.sharding import PartitionSpec as P

W = 256
MESH = pl.DeviceIdType.MESH

N_X, N_C, N_H, N_Y, N_L = 4, 2, 2, 4, 4
CHUNKS = ((0, 48), (48, 48), (96, 48))
N_SEMS = 128


def split_three(v):
    one = v.astype(jnp.bfloat16)
    v = v - one.astype(jnp.float32)
    two = v.astype(jnp.bfloat16)
    three = (v - two.astype(jnp.float32)).astype(jnp.bfloat16)
    return jnp.concatenate([one, two, three], axis=0)


def join_three(v):
    n = v.shape[0] // 3
    return (v[2 * n :] + v[n : 2 * n]) + v[:n]


def ladder_kernel(
    integrals, mask_in, amplitudes_in, first_in, second_in, vir_index, occ_in, partner_in, vir_in, eps_occ_in,
    result1, result2, stage, hi, lo, hi_t, lo_t, cat, par_one, core_one, own, oth1, oth1_peer, oth2, den1, den2, new1,
    new2, pairs, window, mask, amplitudes, other_first, other_second, occ_index, partner, eps_vir, eps_occ, out1,
    out2, *rest
):
    n = len(CHUNKS)
    per = 10
    bufs = [rest[per * k : per * k + per] for k in range(n)]
    stage_sem, window_sem, small_sem, ssem, rsem = rest[per * n :]
    con = lax.axis_index("con")
    res = lax.axis_index("res")
    zh, x, c = con // 8, (con // 2) % 4, con % 2
    y, zl = res // 4, res % 4

    def wrap(v, m):
        return lax.rem(v + m, m)

    def at(zh_=None, x_=None, c_=None, y_=None, zl_=None):
        zh_ = zh if zh_ is None else zh_
        x_ = x if x_ is None else x_
        c_ = c if c_ is None else c_
        y_ = y if y_ is None else y_
        zl_ = zl if zl_ is None else zl_
        return (zh_ * 8 + x_ * 2 + c_, y_ * 4 + zl_)

    used = [0]
    sent = []

    def take(count):
        first = used[0]
        used[0] += count
        return first

    def describe(index, src, dst, device):
        return pltpu.make_async_remote_copy(
            src_ref=src, dst_ref=dst, send_sem=ssem.at[index], recv_sem=rsem.at[index],
            device_id=device, device_id_type=MESH,
        )

    def send(src, dst, device):
        copy = describe(take(1), src, dst, device)
        copy.start()
        sent.append(copy)
        return copy

    peers = (
        [at(zl_=wrap(zl + d, 4)) for d in (1, 2, 3)]
        + [at(y_=wrap(y + d, 4)) for d in (1, 2, 3)]
        + [at(x_=wrap(x + d, 4)) for d in (1, 2, 3)]
        + [at(c_=1 - c), at(zh_=1 - zh)]
    )
    barrier = pltpu.get_barrier_semaphore()
    for peer in peers:
        pl.semaphore_signal(barrier, inc=1, device_id=peer, device_id_type=MESH)

    def bring(i, src, dst):
        copy = pltpu.make_async_copy(src, dst, small_sem.at[i])
        copy.start()
        return copy

    get_partner = bring(0, partner_in, partner.at[0])
    get_amplitudes = bring(1, amplitudes_in, amplitudes)
    get_mask = bring(2, mask_in, mask)
    loads = [
        pltpu.make_async_copy(integrals.at[pl.ds(i * W, W)], stage.at[i], stage_sem.at[i]) for i in range(6)
    ]
    for load in loads:
        load.start()
    get_first = bring(3, first_in, other_first)
    get_second = bring(4, second_in, other_second)
    get_energies = [
        bring(5, occ_in, occ_index), bring(6, vir_in, eps_vir.at[0]), bring(7, eps_occ_in, eps_occ)
    ]
    blocks = (res * 16 + con % 8, res * 16 + 8 + con % 8, con * 16 + res)
    shifts, windows = [], []
    for i, block in enumerate(blocks):
        first = lax.min(block * 96 // 128 * 128, vir_index.shape[1] - 256)
        first = pl.multiple_of(first, 128)
        shifts.append(block * 96 - first)
        windows.append(
            pltpu.make_async_copy(vir_index.at[:, pl.ds(first, 256)], window.at[i], window_sem.at[i])
        )
        windows[i].start()

    half = lax.broadcasted_iota(jnp.int32, (48, 128), 1) < 64

    def map_pairs():
        size = partner.shape[1]
        row = partner[...].astype(jnp.float32)
        col = jnp.broadcast_to(row, (128, size)).T
        col = jnp.concatenate([col] * (size // 128), axis=1)
        down = lax.broadcasted_iota(jnp.int32, (size, size), 0).astype(jnp.float32)
        across = lax.broadcasted_iota(jnp.int32, (size, size), 1)
        wide = across.astype(jnp.float32)
        before = (wide < jnp.minimum(down, col)) & (wide < jnp.broadcast_to(row, (size, size)))
        before = jnp.where(before, 1.0, 0.0).astype(jnp.bfloat16)
        couple = jnp.dot(before, jnp.ones((size, size), jnp.bfloat16), preferred_element_type=jnp.float32)
        place = (64 * (across // 128) + across % 64).astype(jnp.float32)
        sign = jnp.where(down < col, 1.0, -1.0)
        pairs[...] = jnp.where(couple == place, sign, 0.0).astype(jnp.bfloat16)

    def differences(src, dst, copy):
        copy.wait()
        wide = join_three(jnp.dot(split_three(src[...]), pairs[...], preferred_element_type=jnp.float32))
        for k in range(n):
            part = wide[:, 128 * k : 128 * k + 128]
            dst[48 * k : 48 * k + 48, :] = jnp.where(half, part[:48], part[48:])

    def expand(src, dst):
        parts = [src[48 * k : 48 * k + 48, :] for k in range(n)]
        top = jnp.concatenate([jnp.where(half, part, 0.0) for part in parts], axis=1)
        bottom = jnp.concatenate([jnp.where(half, 0.0, part) for part in parts], axis=1)
        both = split_three(0.5 * jnp.concatenate([top, bottom], axis=0))
        dst[...] = join_three(
            lax.dot_general(both, pairs[...], (((1,), (1,)), ((), ())), preferred_element_type=jnp.float32)
        )

    def denominators():
        for copy in get_energies:
            copy.wait()
        occ = occ_index[...]
        picked = jnp.zeros(occ.shape, jnp.float32)
        for i in range(eps_occ.shape[0]):
            picked = jnp.where(occ == i, eps_occ[i], picked)
        energy = jnp.broadcast_to(picked[0:1] + picked[1:2], (16, occ.shape[1]))
        firsts = jnp.maximum(pairs[...].astype(jnp.float32), 0.0).astype(jnp.bfloat16)
        occ_row = join_three(jnp.dot(split_three(energy), firsts, preferred_element_type=jnp.float32))[0:1]
        table = split_three(jnp.broadcast_to(eps_vir[...], (16, eps_vir.shape[1])))
        orbitals = lax.broadcasted_iota(jnp.int32, (eps_vir.shape[1], 256), 0)
        for i in range(3):
            windows[i].wait()
            found = window[i]
            counts = jnp.where(orbitals == found[0:1], 1.0, 0.0) + jnp.where(orbitals == found[1:2], 1.0, 0.0)
            vir = join_three(jnp.dot(table, counts.astype(jnp.bfloat16), preferred_element_type=jnp.float32))
            vir = pltpu.roll(vir, lax.rem(256 - shifts[i], 256), 1)[0:1, 0:128]
            vir = jnp.broadcast_to(vir, (128, 128)).T
            vir = jnp.where(half, vir[:48], vir[48:96])
            for k in range(n):
                value = vir - occ_row[:, 128 * k : 128 * k + 128]
                if i < 2:
                    den1[i, 48 * k : 48 * k + 48, :] = value
                else:
                    den2[48 * k : 48 * k + 48, :] = value

    get_partner.wait()
    map_pairs()
    differences(amplitudes, own, get_amplitudes)
    get_mask.wait()
    pl.semaphore_wait(barrier, len(peers))

    gather_z = [None] * n
    gather_y = [[] for _ in range(n)]

    def spread_y(k, src, dst):
        for d in (2, 1, 3):
            gather_y[k].append(send(src, dst, at(y_=wrap(y + d, 4))))

    def start_gather(k):
        row, rows = CHUNKS[k]
        gat = bufs[k][0]
        mine = own.at[pl.ds(row, rows)]
        gather_z[k] = [send(mine, gat.at[y, d], at(zl_=wrap(zl + d, 4))) for d in (3, 1, 2)]
        spread_y(k, mine, gat.at[y, 0])
        gat[y, 0] = own[row : row + rows]

    def forward(k):
        gat = bufs[k][0]
        for copy in gather_z[k]:
            copy.wait_recv()
        spread_y(k, gat.at[y, pl.ds(1, 3)], gat.at[y, pl.ds(1, 3)])

    def split_tile(i):
        loads[i].wait()

        def body(j, carry):
            cols = pl.ds(pl.multiple_of(j * W, W), W)
            v = stage[i, :, cols] * mask[i, j].astype(jnp.float32)
            h = v.astype(jnp.bfloat16)
            hi[i * W : (i + 1) * W, cols] = h
            lo[i * W : (i + 1) * W, cols] = (v - h.astype(jnp.float32)).astype(jnp.bfloat16)
            return carry

        lax.fori_loop(0, 6, body, 0)

    def turn(first, last):
        def body(t, carry):
            rows = pl.ds(pl.multiple_of((t // 6) * W, W), W)
            cols = pl.ds(pl.multiple_of((t % 6) * W, W), W)
            hi_t[cols, rows] = hi[rows, cols].T
            lo_t[cols, rows] = lo[rows, cols].T
            return carry

        lax.fori_loop(first, last, body, 0)

    def fill_cat(k, b, slab):
        high = slab.astype(jnp.bfloat16).astype(jnp.float32)
        low = slab - high
        top = jnp.where(half, high, pltpu.roll(low, 64, 1))
        bottom = jnp.where(half, pltpu.roll(high, 64, 1), low)
        lanes = slice(128 * k, 128 * k + 128)
        cat[96 * b : 96 * b + 48, lanes] = top.astype(jnp.bfloat16)
        cat[96 * b + 48 : 96 * b + 96, lanes] = bottom.astype(jnp.bfloat16)

    def fold(total):
        total = total + pltpu.roll(total, 64, 1)
        return [
            jnp.where(half, total[96 * p : 96 * p + 48], total[96 * p + 48 : 96 * p + 96]) for p in range(4)
        ]

    core_copies = []

    def fill_first(k):
        gat = bufs[k][0]
        for copy in gather_y[k]:
            copy.wait_recv()
        for b in range(16):
            fill_cat(k, b, gat[b // 4, wrap(zl - b % 4 + 4, 4)])

    def first_product():
        base = take(4)

        def core_copy(it):
            h, xs = it // 2, pl.ds(2 * (it % 2), 2)
            return describe(base + it, par_one.at[1 - c, h, xs], core_one.at[h, xs], at(c_=1 - c))

        def body(it, carry):
            rows = pl.ds(pl.multiple_of(it * 384, 384), 384)
            total = jnp.dot(hi[rows, :], cat[...], preferred_element_type=jnp.float32)
            total = total + jnp.dot(lo[rows, :], cat[...], preferred_element_type=jnp.float32)
            for k in range(n):
                slabs = fold(total[:, 128 * k : 128 * k + 128])
                for p in range(4):
                    par_one[p % 2, it // 2, 2 * (it % 2) + p // 2, 48 * k : 48 * k + 48, :] = slabs[p]
            core_copy(it).start()
            return carry

        lax.fori_loop(0, 4, body, 0)
        core_copies.extend(core_copy(it) for it in range(4))
        sent.extend(core_copies)

    def wait_core():
        for copy in core_copies:
            copy.wait_recv()

    x_copies = [None] * n

    def reduce_x(k):
        xsum, xrecv = bufs[k][1], bufs[k][2]
        here = slice(48 * k, 48 * k + 48)
        x_copies[k] = []
        for d in (2, 1, 3, 0):
            xd = wrap(x + d, 4)
            for h in range(2):
                xsum[xd, h] = par_one[c, h, xd, here, :] + core_one[h, xd, here, :]
            if d:
                x_copies[k].append(send(xsum.at[xd], xrecv.at[d - 1], at(x_=xd)))

    h_copies = [None] * n

    def reduce_h(k):
        xsum, xrecv, hsum, hrecv = bufs[k][1], bufs[k][2], bufs[k][3], bufs[k][4]
        for copy in x_copies[k]:
            copy.wait_recv()
        for h in range(2):
            hsum[h] = (xsum[x, h] + xrecv[1, h]) + (xrecv[0, h] + xrecv[2, h])
        h_copies[k] = send(hsum, hrecv, at(zh_=1 - zh))

    ux_copies = [None] * n
    uc_copies = [None] * n

    def forward_core(k, first, count):
        ug = bufs[k][5]
        piece = ug.at[c, pl.ds(first, count)]
        uc_copies[k].append(send(piece, piece, at(c_=1 - c)))

    def update_one(k):
        row, rows = CHUNKS[k]
        hsum, hrecv, ug = bufs[k][3], bufs[k][4], bufs[k][5]
        h_copies[k].wait_recv()
        here = slice(row, row + rows)
        both = []
        for h in range(2):
            other = jnp.where(zh == h, oth1[here, :], oth1_peer[here, :])
            value = (other + (hsum[h] + hrecv[h])) / den1[h, here, :]
            ug[c, 0, h] = value
            both.append(value)
        ux_copies[k] = []
        uc_copies[k] = []
        for d in (2, 1, 3):
            ux_copies[k].append(send(ug.at[c, 0], ug.at[c, d], at(x_=wrap(x + d, 4))))
        forward_core(k, 0, 1)
        new1[here, :] = jnp.where(zh == 0, both[0], both[1])

    def pass_core(k):
        for copy in ux_copies[k]:
            copy.wait_recv()
        forward_core(k, 1, 3)

    y_copies = [None] * n

    def second_product(k):
        ug, par, yrecv = bufs[k][5], bufs[k][6], bufs[k][7]
        for copy in uc_copies[k]:
            copy.wait_recv()
        for b in range(16):
            fill_cat(k, b, ug[b % 2, wrap(x - (b // 2) % 4 + 4, 4), b // 8])
        base = take(3)

        def y_copy(it):
            yd = wrap(y + 1 + it, 4)
            return describe(base + it, par.at[yd], yrecv.at[it], at(y_=yd))

        def body(it, carry):
            yd = wrap(y + 1 + it, 4)
            rows = pl.ds(pl.multiple_of(yd * 384, 384), 384)
            operand = cat[:, 128 * k : 128 * k + 128]
            total = jnp.dot(hi_t[rows, :], operand, preferred_element_type=jnp.float32)
            slabs = fold(total + jnp.dot(lo_t[rows, :], operand, preferred_element_type=jnp.float32))
            for p in range(4):
                par[yd, p] = slabs[p]

            @pl.when(it < 3)
            def _():
                y_copy(it).start()

            return carry

        lax.fori_loop(0, 4, body, 0)
        y_copies[k] = [y_copy(it) for it in range(3)]
        sent.extend(y_copies[k])

    l_copies = [None] * n

    def reduce_l(k):
        par, yrecv, ysum, lrecv = bufs[k][6], bufs[k][7], bufs[k][8], bufs[k][9]
        for copy in y_copies[k]:
            copy.wait_recv()
        l_copies[k] = []
        for d in (2, 1, 3, 0):
            ld = wrap(zl + d, 4)
            ysum[ld] = (par[y, ld] + yrecv[0, ld]) + (yrecv[1, ld] + yrecv[2, ld])
            if d:
                l_copies[k].append(send(ysum.at[ld], lrecv.at[d - 1], at(zl_=ld)))

    def update_two(k):
        row, rows = CHUNKS[k]
        ysum, lrecv = bufs[k][8], bufs[k][9]
        for copy in l_copies[k]:
            copy.wait_recv()
        here = slice(row, row + rows)
        ladder = (ysum[zl] + lrecv[0]) + (lrecv[1] + lrecv[2])
        new2[here, :] = (oth2[here, :] + ladder) / den2[here, :]

    start_gather(0)
    start_gather(1)
    start_gather(2)
    differences(other_first, oth1, get_first)
    other_copy = send(oth1, oth1_peer, at(zh_=1 - zh))
    split_tile(0)
    split_tile(1)
    forward(0)
    split_tile(2)
    forward(1)
    split_tile(3)
    forward(2)
    split_tile(4)
    split_tile(5)
    denominators()
    fill_first(0)
    fill_first(1)
    fill_first(2)
    first_product()
    turn(0, 6)
    wait_core()
    reduce_x(0)
    reduce_x(1)
    reduce_x(2)
    turn(6, 18)
    other_copy.wait_recv()
    reduce_h(0)
    reduce_h(1)
    reduce_h(2)
    turn(18, 36)
    update_one(0)
    update_one(1)
    update_one(2)
    pass_core(0)
    pass_core(1)
    pass_core(2)
    second_product(0)
    second_product(1)
    second_product(2)
    differences(other_second, oth2, get_second)
    expand(new1, out1)
    give1 = bring(8, out1, result1)
    reduce_l(0)
    reduce_l(1)
    reduce_l(2)
    update_two(0)
    update_two(1)
    update_two(2)
    expand(new2, out2)
    give2 = bring(9, out2, result2)
    give1.wait()
    give2.wait()
    for copy in sent:
        copy.wait_send()


def deliver_kernel(first, second, out1, out2, held, sems):
    into = [pltpu.make_async_copy(src, held.at[i], sems.at[i]) for i, src in enumerate((first, second))]
    away = [pltpu.make_async_copy(held.at[i], dst, sems.at[2 + i]) for i, dst in enumerate((out1, out2))]
    for copy in into:
        copy.start()
    for i in range(2):
        into[i].wait()
        away[i].start()
    for copy in away:
        copy.wait()


def per_device(
    integrals,
    tile_mask,
    amplitudes,
    other_first,
    other_second,
    vir_index,
    occ_index,
    partner,
    eps_vir,
    eps_occ,
):
    f32, bf16 = jnp.float32, jnp.bfloat16
    side = integrals.shape[0]
    packed = (144, 128)
    scratch = [pltpu.VMEM((6, W, side), f32)]
    scratch += [pltpu.VMEM((side, side), bf16)] * 4
    scratch += [pltpu.VMEM((side, 384), bf16), pltpu.VMEM((2, 2, 4) + packed, f32), pltpu.VMEM((2, 4) + packed, f32)]
    scratch += [pltpu.VMEM(packed, f32)] * 4
    scratch += [pltpu.VMEM((2,) + packed, f32)]
    scratch += [pltpu.VMEM(packed, f32)] * 3
    scratch += [pltpu.VMEM((384, 384), bf16), pltpu.VMEM((3, 2, 256), jnp.int32)]
    scratch += [pltpu.SMEM(tile_mask.shape, jnp.int32)] + [pltpu.VMEM(amplitudes.shape, f32)] * 3
    scratch += [pltpu.VMEM(occ_index.shape, jnp.int32), pltpu.VMEM((1,) + partner.shape, jnp.int32)]
    scratch += [pltpu.VMEM((1,) + eps_vir.shape, f32), pltpu.SMEM(eps_occ.shape, f32)]
    scratch += [pltpu.VMEM(amplitudes.shape, f32)] * 2
    for _, rows in CHUNKS:
        for lead in (
            (4, 4), (4, 2), (3, 2), (2,), (2,), (2, 4, 2), (4, 4), (3, 4), (4,), (3,)
        ):
            scratch.append(pltpu.VMEM(lead + (rows, 128), f32))
    scratch += [
        pltpu.SemaphoreType.DMA((6,)),
        pltpu.SemaphoreType.DMA((3,)),
        pltpu.SemaphoreType.DMA((10,)),
        pltpu.SemaphoreType.DMA((N_SEMS,)),
        pltpu.SemaphoreType.DMA((N_SEMS,)),
    ]
    hbm = pl.BlockSpec(memory_space=pl.ANY)
    shapes = [jax.ShapeDtypeStruct(amplitudes.shape, f32)] * 2
    first, second = pl.pallas_call(
        ladder_kernel,
        out_shape=shapes,
        in_specs=[hbm] * 10,
        out_specs=[hbm] * 2,
        scratch_shapes=scratch,
        compiler_params=pltpu.CompilerParams(
            collective_id=0, has_side_effects=True, vmem_limit_bytes=56 * 1024 * 1024
        ),
        name="ladders",
    )(
        integrals, tile_mask, amplitudes, other_first, other_second, vir_index, occ_index, partner, eps_vir, eps_occ
    )
    return pl.pallas_call(
        deliver_kernel,
        out_shape=shapes,
        in_specs=[hbm] * 2,
        out_specs=[hbm] * 2,
        scratch_shapes=[pltpu.VMEM((2,) + amplitudes.shape, f32), pltpu.SemaphoreType.DMA((4,))],
        name="deliver",
    )(first, second)


def solution(mesh):
    return jax.shard_map(
        per_device,
        mesh=mesh,
        in_specs=(
            P("res", "con"),
            P("res", "con"),
            P(("con", "res"), None),
            P(("res", "con"), None),
            P(("con", "res"), None),
            P(),
            P(),
            P(),
            P(),
            P(),
        ),
        out_specs=(P(("res", "con"), None), P(("con", "res"), None)),
        check_vma=False,
    )
```

```python
import jax
import jax.numpy as jnp
from jax import lax
from jax.experimental import pallas as pl
from jax.experimental.pallas import tpu as pltpu
from jax.sharding import PartitionSpec as P

W = 256
MESH = pl.DeviceIdType.MESH

N_X, N_C, N_H, N_Y, N_L = 4, 2, 2, 4, 4
CHUNKS = ((0, 48), (48, 48), (96, 48))
N_SEMS = 128


def split_three(v):
    one = v.astype(jnp.bfloat16)
    v = v - one.astype(jnp.float32)
    two = v.astype(jnp.bfloat16)
    three = (v - two.astype(jnp.float32)).astype(jnp.bfloat16)
    return jnp.concatenate([one, two, three], axis=0)


def join_three(v):
    n = v.shape[0] // 3
    return (v[2 * n :] + v[n : 2 * n]) + v[:n]


def ladder_kernel(
    integrals, mask_in, amplitudes_in, first_in, second_in, vir_index, occ_in, partner_in, vir_in, eps_occ_in,
    result1, result2, stage, hi, lo, hi_t, lo_t, left, own, oth1, oth1_peer, oth2, den1, den2, new1,
    new2, pairs, window, mask, amplitudes, other_first, other_second, occ_index, partner, eps_vir, eps_occ, out1,
    out2, *rest
):
    n = len(CHUNKS)
    per = 12
    bufs = [rest[per * k : per * k + per] for k in range(n)]
    stage_sem, window_sem, small_sem, ssem, rsem = rest[per * n :]
    con = lax.axis_index("con")
    res = lax.axis_index("res")
    zh, x, c = con // 8, (con // 2) % 4, con % 2
    y, zl = res // 4, res % 4

    def wrap(v, m):
        return lax.rem(v + m, m)

    def at(zh_=None, x_=None, c_=None, y_=None, zl_=None):
        zh_ = zh if zh_ is None else zh_
        x_ = x if x_ is None else x_
        c_ = c if c_ is None else c_
        y_ = y if y_ is None else y_
        zl_ = zl if zl_ is None else zl_
        return (zh_ * 8 + x_ * 2 + c_, y_ * 4 + zl_)

    used = [0]
    sent = []

    def take(count):
        first = used[0]
        used[0] += count
        return first

    def describe(index, src, dst, device):
        return pltpu.make_async_remote_copy(
            src_ref=src, dst_ref=dst, send_sem=ssem.at[index], recv_sem=rsem.at[index],
            device_id=device, device_id_type=MESH,
        )

    def send(src, dst, device):
        copy = describe(take(1), src, dst, device)
        copy.start()
        sent.append(copy)
        return copy

    peers = (
        [at(zl_=wrap(zl + d, 4)) for d in (1, 2, 3)]
        + [at(y_=wrap(y + d, 4)) for d in (1, 2, 3)]
        + [at(x_=wrap(x + d, 4)) for d in (1, 2, 3)]
        + [at(c_=1 - c), at(zh_=1 - zh)]
    )
    barrier = pltpu.get_barrier_semaphore()
    for peer in peers:
        pl.semaphore_signal(barrier, inc=1, device_id=peer, device_id_type=MESH)

    def bring(i, src, dst):
        copy = pltpu.make_async_copy(src, dst, small_sem.at[i])
        copy.start()
        return copy

    get_partner = bring(0, partner_in, partner.at[0])
    get_amplitudes = bring(1, amplitudes_in, amplitudes)
    get_mask = bring(2, mask_in, mask)
    def starts(t):
        return [96 * (4 * (t % 4) + p) + 48 * (t // 4) for p in range(4)]

    loads = [
        [
            pltpu.make_async_copy(
                integrals.at[pl.ds(first, 48)], stage.at[t, pl.ds(48 * p, 48)], stage_sem.at[t, p]
            )
            for p, first in enumerate(starts(t))
        ]
        for t in range(8)
    ]
    for group in loads:
        for load in group:
            load.start()
    get_first = bring(3, first_in, other_first)
    get_second = bring(4, second_in, other_second)
    get_energies = [
        bring(5, occ_in, occ_index), bring(6, vir_in, eps_vir.at[0]), bring(7, eps_occ_in, eps_occ)
    ]
    blocks = (res * 16 + con % 8, res * 16 + 8 + con % 8, con * 16 + res)
    shifts, windows = [], []
    for i, block in enumerate(blocks):
        first = lax.min(block * 96 // 128 * 128, vir_index.shape[1] - 256)
        first = pl.multiple_of(first, 128)
        shifts.append(block * 96 - first)
        windows.append(
            pltpu.make_async_copy(vir_index.at[:, pl.ds(first, 256)], window.at[i], window_sem.at[i])
        )
        windows[i].start()

    half = lax.broadcasted_iota(jnp.int32, (48, 128), 1) < 64

    def map_pairs():
        size = partner.shape[1]
        row = partner[...].astype(jnp.float32)
        col = jnp.broadcast_to(row, (128, size)).T
        col = jnp.concatenate([col] * (size // 128), axis=1)
        down = lax.broadcasted_iota(jnp.int32, (size, size), 0).astype(jnp.float32)
        across = lax.broadcasted_iota(jnp.int32, (size, size), 1)
        wide = across.astype(jnp.float32)
        before = (wide < jnp.minimum(down, col)) & (wide < jnp.broadcast_to(row, (size, size)))
        before = jnp.where(before, 1.0, 0.0).astype(jnp.bfloat16)
        couple = jnp.dot(before, jnp.ones((size, size), jnp.bfloat16), preferred_element_type=jnp.float32)
        place = (64 * (across // 128) + across % 64).astype(jnp.float32)
        sign = jnp.where(down < col, 1.0, -1.0)
        pairs[...] = jnp.where(couple == place, sign, 0.0).astype(jnp.bfloat16)

    def differences(src, dst, copy):
        copy.wait()
        wide = join_three(jnp.dot(split_three(src[...]), pairs[...], preferred_element_type=jnp.float32))
        for k in range(n):
            part = wide[:, 128 * k : 128 * k + 128]
            dst[48 * k : 48 * k + 48, :] = jnp.where(half, part[:48], part[48:])

    def expand(src, dst):
        parts = [src[48 * k : 48 * k + 48, :] for k in range(n)]
        top = jnp.concatenate([jnp.where(half, part, 0.0) for part in parts], axis=1)
        bottom = jnp.concatenate([jnp.where(half, 0.0, part) for part in parts], axis=1)
        both = split_three(0.5 * jnp.concatenate([top, bottom], axis=0))
        dst[...] = join_three(
            lax.dot_general(both, pairs[...], (((1,), (1,)), ((), ())), preferred_element_type=jnp.float32)
        )

    def denominators():
        for copy in get_energies:
            copy.wait()
        occ = occ_index[...]
        picked = jnp.zeros(occ.shape, jnp.float32)
        for i in range(eps_occ.shape[0]):
            picked = jnp.where(occ == i, eps_occ[i], picked)
        energy = jnp.broadcast_to(picked[0:1] + picked[1:2], (16, occ.shape[1]))
        firsts = jnp.maximum(pairs[...].astype(jnp.float32), 0.0).astype(jnp.bfloat16)
        occ_row = join_three(jnp.dot(split_three(energy), firsts, preferred_element_type=jnp.float32))[0:1]
        table = split_three(jnp.broadcast_to(eps_vir[...], (16, eps_vir.shape[1])))
        orbitals = lax.broadcasted_iota(jnp.int32, (eps_vir.shape[1], 256), 0)
        for i in range(3):
            windows[i].wait()
            found = window[i]
            counts = jnp.where(orbitals == found[0:1], 1.0, 0.0) + jnp.where(orbitals == found[1:2], 1.0, 0.0)
            vir = join_three(jnp.dot(table, counts.astype(jnp.bfloat16), preferred_element_type=jnp.float32))
            vir = pltpu.roll(vir, lax.rem(256 - shifts[i], 256), 1)[0:1, 0:128]
            vir = jnp.broadcast_to(vir, (128, 128)).T
            vir = jnp.where(half, vir[:48], vir[48:96])
            for k in range(n):
                value = vir - occ_row[:, 128 * k : 128 * k + 128]
                if i < 2:
                    den1[i, 48 * k : 48 * k + 48, :] = value
                else:
                    den2[48 * k : 48 * k + 48, :] = value

    get_partner.wait()
    map_pairs()
    differences(amplitudes, own, get_amplitudes)
    get_mask.wait()
    pl.semaphore_wait(barrier, len(peers))

    gather_z = [None] * n
    gather_y = [[] for _ in range(n)]

    def spread_y(k, src, dst):
        for d in (2, 1, 3):
            gather_y[k].append(send(src, dst, at(y_=wrap(y + d, 4))))

    def start_gather(k):
        row, rows = CHUNKS[k]
        gat = bufs[k][0]
        mine = own.at[pl.ds(row, rows)]
        gather_z[k] = [send(mine, gat.at[y, d], at(zl_=wrap(zl + d, 4))) for d in (3, 1, 2)]
        spread_y(k, mine, gat.at[y, 0])
        gat[y, 0] = own[row : row + rows]

    def forward(k):
        gat = bufs[k][0]
        for copy in gather_z[k]:
            copy.wait_recv()
        spread_y(k, gat.at[y, pl.ds(1, 3)], gat.at[y, pl.ds(1, 3)])

    def split_tile(t):
        for load in loads[t]:
            load.wait()
        pieces = []
        for p, first in enumerate(starts(t)):
            cut = min(48, W * (first // W + 1) - first)
            pieces.append((48 * p, cut, first // W))
            if cut < 48:
                pieces.append((48 * p + cut, 48 - cut, first // W + 1))

        def body(j, carry):
            cols = pl.ds(pl.multiple_of(j * W, W), W)
            for at_row, count, tile in pieces:
                v = stage[t, at_row : at_row + count, cols] * mask[tile, j].astype(jnp.float32)
                h = v.astype(jnp.bfloat16)
                rows = slice(192 * t + at_row, 192 * t + at_row + count)
                hi[rows, cols] = h
                lo[rows, cols] = (v - h.astype(jnp.float32)).astype(jnp.bfloat16)
            return carry

        lax.fori_loop(0, 6, body, 0)

    def turn_out(first, last):
        def body(t, carry):
            q = t % 4
            lanes = pl.ds(pl.multiple_of((t // 4) * W, W), W)
            cols = pl.ds(pl.multiple_of(q * 384, 384), 384)
            for src, dst in ((hi, hi_t), (lo, lo_t)):
                turned = src[lanes, cols].T
                for p in range(4):
                    for h in range(2):
                        rows = pl.ds(pl.multiple_of(768 * h + 192 * q + 48 * p, 16), 48)
                        dst[rows, lanes] = turned[96 * p + 48 * h : 96 * p + 48 * h + 48]
            return carry

        lax.fori_loop(first, last, body, 0)

    def turn_back(first, last):
        def body(t, carry):
            rows = pl.ds(pl.multiple_of((t // 6) * W, W), W)
            cols = pl.ds(pl.multiple_of((t % 6) * W, W), W)
            hi[cols, rows] = hi_t[rows, cols].T
            lo[cols, rows] = lo_t[rows, cols].T
            return carry

        lax.fori_loop(first, last, body, 0)

    def fill_left(slot, slab):
        for i in range(2):
            turned = jnp.concatenate([slab(8 * i + p) for p in range(8)], axis=0).T
            high = turned.astype(jnp.bfloat16)
            low = (turned - high.astype(jnp.float32)).astype(jnp.bfloat16)
            lanes = slice(384 * i, 384 * i + 384)
            for part in range(2):
                left[slot, part, 0:64, lanes] = high[64 * part : 64 * part + 64]
                left[slot, part, 64:128, lanes] = low[64 * part : 64 * part + 64]

    def product(slot, high, low, i):
        parts = []
        for part in range(2):
            lanes = pl.ds(pl.multiple_of(768 * part + 384 * i, 128), 384)
            both = jnp.dot(left[slot, 0], high[0:768, lanes], preferred_element_type=jnp.float32)
            both = both + jnp.dot(left[slot, 1], high[768:1536, lanes], preferred_element_type=jnp.float32)
            rest_ = jnp.dot(left[slot, 0, 0:64], low[0:768, lanes], preferred_element_type=jnp.float32)
            rest_ = rest_ + jnp.dot(left[slot, 1, 0:64], low[768:1536, lanes], preferred_element_type=jnp.float32)
            parts.append(both[0:64] + (both[64:128] + rest_))
        return jnp.concatenate(parts, axis=0).T

    core_copies = [None] * n

    def first_product(k):
        gat, par, corr = bufs[k][0], bufs[k][1], bufs[k][2]
        for copy in gather_y[k]:
            copy.wait_recv()
        fill_left(k, lambda b: gat[b // 4, wrap(zl - b % 4 + 4, 4)])
        base = take(2)

        def core_copy(i):
            return describe(base + i, par.at[1 - c, i], corr.at[i], at(c_=1 - c))

        def body(i, carry):
            packed = product(k, hi_t, lo_t, i)
            for p in range(8):
                par[p % 2, i, p // 2] = packed[48 * p : 48 * p + 48]
            core_copy(i).start()
            return carry

        lax.fori_loop(0, 2, body, 0)
        core_copies[k] = [core_copy(i) for i in range(2)]
        sent.extend(core_copies[k])

    x_copies = [None] * n

    def reduce_x(k):
        par, corr, xsum, xrecv = bufs[k][1], bufs[k][2], bufs[k][3], bufs[k][4]
        for copy in core_copies[k]:
            copy.wait_recv()
        x_copies[k] = []
        for d in (2, 1, 3, 0):
            xd = wrap(x + d, 4)
            for h in range(2):
                xsum[xd, h] = par[c, h, xd] + corr[h, xd]
            if d:
                x_copies[k].append(send(xsum.at[xd], xrecv.at[d - 1], at(x_=xd)))

    h_copies = [None] * n

    def reduce_h(k):
        xsum, xrecv, hsum, hrecv = bufs[k][3], bufs[k][4], bufs[k][5], bufs[k][6]
        for copy in x_copies[k]:
            copy.wait_recv()
        for h in range(2):
            hsum[h] = (xsum[x, h] + xrecv[1, h]) + (xrecv[0, h] + xrecv[2, h])
        h_copies[k] = send(hsum, hrecv, at(zh_=1 - zh))

    ux_copies = [None] * n
    uc_copies = [None] * n

    def forward_core(k, first, count):
        ug = bufs[k][7]
        piece = ug.at[c, pl.ds(first, count)]
        uc_copies[k].append(send(piece, piece, at(c_=1 - c)))

    def update_one(k):
        row, rows = CHUNKS[k]
        hsum, hrecv, ug = bufs[k][5], bufs[k][6], bufs[k][7]
        h_copies[k].wait_recv()
        here = slice(row, row + rows)
        both = []
        for h in range(2):
            other = jnp.where(zh == h, oth1[here, :], oth1_peer[here, :])
            value = (other + (hsum[h] + hrecv[h])) / den1[h, here, :]
            ug[c, 0, h] = value
            both.append(value)
        ux_copies[k] = []
        uc_copies[k] = []
        for d in (2, 1, 3):
            ux_copies[k].append(send(ug.at[c, 0], ug.at[c, d], at(x_=wrap(x + d, 4))))
        forward_core(k, 0, 1)
        new1[here, :] = jnp.where(zh == 0, both[0], both[1])

    def pass_core(k):
        for copy in ux_copies[k]:
            copy.wait_recv()
        forward_core(k, 1, 3)

    y_copies = [None] * n

    def second_product(k):
        ug, par, yrecv = bufs[k][7], bufs[k][8], bufs[k][9]
        for copy in uc_copies[k]:
            copy.wait_recv()
        fill_left(3 + k, lambda b: ug[b % 2, wrap(x - (b // 2) % 4 + 4, 4), b // 8])
        base = take(3)

        def y_copy(yd, d):
            return describe(base + d - 1, par.at[yd], yrecv.at[d - 1], at(y_=yd))

        def body(i, carry):
            packed = product(3 + k, hi, lo, i)
            for p in range(8):
                par[2 * i + p // 4, p % 4] = packed[48 * p : 48 * p + 48]
            for e in range(2):
                yd = 2 * i + e
                d = lax.rem(yd - y + 4, 4)

                @pl.when(d > 0)
                def _():
                    y_copy(yd, d).start()

            return carry

        lax.fori_loop(0, 2, body, 0)
        y_copies[k] = [y_copy(wrap(y + d, 4), d) for d in (1, 2, 3)]
        sent.extend(y_copies[k])

    l_copies = [None] * n

    def reduce_l(k):
        par, yrecv, ysum, lrecv = bufs[k][8], bufs[k][9], bufs[k][10], bufs[k][11]
        for copy in y_copies[k]:
            copy.wait_recv()
        l_copies[k] = []
        for d in (2, 1, 3, 0):
            ld = wrap(zl + d, 4)
            ysum[ld] = (par[y, ld] + yrecv[0, ld]) + (yrecv[1, ld] + yrecv[2, ld])
            if d:
                l_copies[k].append(send(ysum.at[ld], lrecv.at[d - 1], at(zl_=ld)))

    def update_two(k):
        row, rows = CHUNKS[k]
        ysum, lrecv = bufs[k][10], bufs[k][11]
        for copy in l_copies[k]:
            copy.wait_recv()
        here = slice(row, row + rows)
        ladder = (ysum[zl] + lrecv[0]) + (lrecv[1] + lrecv[2])
        new2[here, :] = (oth2[here, :] + ladder) / den2[here, :]

    start_gather(0)
    split_tile(0)
    split_tile(1)
    start_gather(1)
    split_tile(2)
    split_tile(3)
    forward(0)
    start_gather(2)
    split_tile(4)
    split_tile(5)
    forward(1)
    split_tile(6)
    split_tile(7)
    turn_out(0, 24)
    forward(2)
    differences(other_first, oth1, get_first)
    other_copy = send(oth1, oth1_peer, at(zh_=1 - zh))
    first_product(0)
    denominators()
    reduce_x(0)
    first_product(1)
    reduce_h(0)
    reduce_x(1)
    first_product(2)
    turn_back(0, 18)
    other_copy.wait_recv()
    update_one(0)
    reduce_h(1)
    reduce_x(2)
    turn_back(18, 36)
    pass_core(0)
    update_one(1)
    reduce_h(2)
    second_product(0)
    pass_core(1)
    update_one(2)
    second_product(1)
    pass_core(2)
    reduce_l(0)
    second_product(2)
    differences(other_second, oth2, get_second)
    expand(new1, out1)
    give1 = bring(8, out1, result1)
    reduce_l(1)
    update_two(0)
    reduce_l(2)
    update_two(1)
    update_two(2)
    expand(new2, out2)
    give2 = bring(9, out2, result2)
    give1.wait()
    give2.wait()
    for copy in sent:
        copy.wait_send()


def deliver_kernel(first, second, out1, out2, held, sems):
    into = [pltpu.make_async_copy(src, held.at[i], sems.at[i]) for i, src in enumerate((first, second))]
    away = [pltpu.make_async_copy(held.at[i], dst, sems.at[2 + i]) for i, dst in enumerate((out1, out2))]
    for copy in into:
        copy.start()
    for i in range(2):
        into[i].wait()
        away[i].start()
    for copy in away:
        copy.wait()


def per_device(
    integrals,
    tile_mask,
    amplitudes,
    other_first,
    other_second,
    vir_index,
    occ_index,
    partner,
    eps_vir,
    eps_occ,
):
    f32, bf16 = jnp.float32, jnp.bfloat16
    side = integrals.shape[0]
    packed = (144, 128)
    scratch = [pltpu.VMEM((8, 192, side), f32)]
    scratch += [pltpu.VMEM((side, side), bf16)] * 4
    scratch += [pltpu.VMEM((6, 2, 128, side // 2), bf16)]
    scratch += [pltpu.VMEM(packed, f32)] * 4
    scratch += [pltpu.VMEM((2,) + packed, f32)]
    scratch += [pltpu.VMEM(packed, f32)] * 3
    scratch += [pltpu.VMEM((384, 384), bf16), pltpu.VMEM((3, 2, 256), jnp.int32)]
    scratch += [pltpu.SMEM(tile_mask.shape, jnp.int32)] + [pltpu.VMEM(amplitudes.shape, f32)] * 3
    scratch += [pltpu.VMEM(occ_index.shape, jnp.int32), pltpu.VMEM((1,) + partner.shape, jnp.int32)]
    scratch += [pltpu.VMEM((1,) + eps_vir.shape, f32), pltpu.SMEM(eps_occ.shape, f32)]
    scratch += [pltpu.VMEM(amplitudes.shape, f32)] * 2
    for _, rows in CHUNKS:
        for lead in (
            (4, 4), (2, 2, 4), (2, 4), (4, 2), (3, 2), (2,), (2,), (2, 4, 2), (4, 4), (3, 4), (4,), (3,)
        ):
            scratch.append(pltpu.VMEM(lead + (rows, 128), f32))
    scratch += [
        pltpu.SemaphoreType.DMA((8, 4)),
        pltpu.SemaphoreType.DMA((3,)),
        pltpu.SemaphoreType.DMA((10,)),
        pltpu.SemaphoreType.DMA((N_SEMS,)),
        pltpu.SemaphoreType.DMA((N_SEMS,)),
    ]
    hbm = pl.BlockSpec(memory_space=pl.ANY)
    shapes = [jax.ShapeDtypeStruct(amplitudes.shape, f32)] * 2
    first, second = pl.pallas_call(
        ladder_kernel,
        out_shape=shapes,
        in_specs=[hbm] * 10,
        out_specs=[hbm] * 2,
        scratch_shapes=scratch,
        compiler_params=pltpu.CompilerParams(
            collective_id=0, has_side_effects=True, vmem_limit_bytes=56 * 1024 * 1024
        ),
        name="ladders",
    )(
        integrals, tile_mask, amplitudes, other_first, other_second, vir_index, occ_index, partner, eps_vir, eps_occ
    )
    return pl.pallas_call(
        deliver_kernel,
        out_shape=shapes,
        in_specs=[hbm] * 2,
        out_specs=[hbm] * 2,
        scratch_shapes=[pltpu.VMEM((2,) + amplitudes.shape, f32), pltpu.SemaphoreType.DMA((4,))],
        name="deliver",
    )(first, second)


def solution(mesh):
    return jax.shard_map(
        per_device,
        mesh=mesh,
        in_specs=(
            P("res", "con"),
            P("res", "con"),
            P(("con", "res"), None),
            P(("res", "con"), None),
            P(("con", "res"), None),
            P(),
            P(),
            P(),
            P(),
            P(),
        ),
        out_specs=(P(("res", "con"), None), P(("con", "res"), None)),
        check_vma=False,
    )
```

```python
import jax
import jax.numpy as jnp
from jax import lax
from jax.experimental import pallas as pl
from jax.experimental.pallas import tpu as pltpu
from jax.sharding import PartitionSpec as P

W = 256
MESH = pl.DeviceIdType.MESH

N_X, N_C, N_H, N_Y, N_L = 4, 2, 2, 4, 4
CHUNKS = ((0, 48), (48, 48), (96, 48))
N_SEMS = 128
LATE = (1, 2)


def split_three(v):
    one = v.astype(jnp.bfloat16)
    v = v - one.astype(jnp.float32)
    two = v.astype(jnp.bfloat16)
    three = (v - two.astype(jnp.float32)).astype(jnp.bfloat16)
    return jnp.concatenate([one, two, three], axis=0)


def join_three(v):
    n = v.shape[0] // 3
    return (v[2 * n :] + v[n : 2 * n]) + v[:n]


def ladder_kernel(
    integrals, mask_in, amplitudes_in, first_in, second_in, vir_index, occ_in, partner_in, vir_in, eps_occ_in,
    result1, result2, stage, hi, lo, hi_t, lo_t, left, own, oth1, oth1_peer, oth2, den1, den2, new1,
    new2, pairs, window, mask, amplitudes, other_first, other_second, occ_index, partner, eps_vir, eps_occ, *rest
):
    n = len(CHUNKS)
    per = 12
    bufs = [rest[per * k : per * k + per] for k in range(n)]
    stage_sem, window_sem, small_sem, ssem, rsem = rest[per * n :]
    con = lax.axis_index("con")
    res = lax.axis_index("res")
    zh, x, c = con // 8, (con // 2) % 4, con % 2
    y, zl = res // 4, res % 4

    def wrap(v, m):
        return lax.rem(v + m, m)

    def at(zh_=None, x_=None, c_=None, y_=None, zl_=None):
        zh_ = zh if zh_ is None else zh_
        x_ = x if x_ is None else x_
        c_ = c if c_ is None else c_
        y_ = y if y_ is None else y_
        zl_ = zl if zl_ is None else zl_
        return (zh_ * 8 + x_ * 2 + c_, y_ * 4 + zl_)

    used = [0]
    sent = []

    def take(count):
        first = used[0]
        used[0] += count
        return first

    def describe(index, src, dst, device):
        return pltpu.make_async_remote_copy(
            src_ref=src, dst_ref=dst, send_sem=ssem.at[index], recv_sem=rsem.at[index],
            device_id=device, device_id_type=MESH,
        )

    def send(src, dst, device):
        copy = describe(take(1), src, dst, device)
        copy.start()
        sent.append(copy)
        return copy

    peers = (
        [at(zl_=wrap(zl + d, 4)) for d in (1, 2, 3)]
        + [at(y_=wrap(y + d, 4)) for d in (1, 2, 3)]
        + [at(x_=wrap(x + d, 4)) for d in (1, 2, 3)]
        + [at(c_=1 - c), at(zh_=1 - zh)]
    )
    barrier = pltpu.get_barrier_semaphore()
    for peer in peers:
        pl.semaphore_signal(barrier, inc=1, device_id=peer, device_id_type=MESH)

    def bring(i, src, dst):
        copy = pltpu.make_async_copy(src, dst, small_sem.at[i])
        copy.start()
        return copy

    get_partner = bring(0, partner_in, partner.at[0])
    get_amplitudes = bring(1, amplitudes_in, amplitudes)
    get_mask = bring(2, mask_in, mask)
    def starts(t):
        return [96 * (4 * (t % 4) + p) + 48 * (t // 4) for p in range(4)]

    loads = [
        [
            pltpu.make_async_copy(
                integrals.at[pl.ds(first, 48)], stage.at[t, pl.ds(48 * p, 48)], stage_sem.at[t, p]
            )
            for p, first in enumerate(starts(t))
        ]
        for t in range(8)
    ]
    for group in loads:
        for load in group:
            load.start()
    get_first = bring(3, first_in, other_first)
    get_second = bring(4, second_in, other_second)
    get_energies = [
        bring(5, occ_in, occ_index), bring(6, vir_in, eps_vir.at[0]), bring(7, eps_occ_in, eps_occ)
    ]
    blocks = (res * 16 + con % 8, res * 16 + 8 + con % 8, con * 16 + res)
    shifts, windows = [], []
    for i, block in enumerate(blocks):
        first = lax.min(block * 96 // 128 * 128, vir_index.shape[1] - 256)
        first = pl.multiple_of(first, 128)
        shifts.append(block * 96 - first)
        windows.append(
            pltpu.make_async_copy(vir_index.at[:, pl.ds(first, 256)], window.at[i], window_sem.at[i])
        )
        windows[i].start()

    half = lax.broadcasted_iota(jnp.int32, (48, 128), 1) < 64

    def map_pairs():
        size = partner.shape[1]
        row = partner[...].astype(jnp.float32)
        col = jnp.broadcast_to(row, (128, size)).T
        col = jnp.concatenate([col] * (size // 128), axis=1)
        down = lax.broadcasted_iota(jnp.int32, (size, size), 0).astype(jnp.float32)
        across = lax.broadcasted_iota(jnp.int32, (size, size), 1)
        wide = across.astype(jnp.float32)
        before = (wide < jnp.minimum(down, col)) & (wide < jnp.broadcast_to(row, (size, size)))
        before = jnp.where(before, 1.0, 0.0).astype(jnp.bfloat16)
        couple = jnp.dot(before, jnp.ones((size, size), jnp.bfloat16), preferred_element_type=jnp.float32)
        place = (64 * (across // 128) + across % 64).astype(jnp.float32)
        sign = jnp.where(down < col, 1.0, -1.0)
        pairs[...] = jnp.where(couple == place, sign, 0.0).astype(jnp.bfloat16)

    def differences(src, dst, copy):
        copy.wait()
        wide = join_three(jnp.dot(split_three(src[...]), pairs[...], preferred_element_type=jnp.float32))
        for k in range(n):
            part = wide[:, 128 * k : 128 * k + 128]
            dst[48 * k : 48 * k + 48, :] = jnp.where(half, part[:48], part[48:])

    def expand(src, dst):
        parts = [src[48 * k : 48 * k + 48, :] for k in range(n)]
        top = jnp.concatenate([jnp.where(half, part, 0.0) for part in parts], axis=1)
        bottom = jnp.concatenate([jnp.where(half, 0.0, part) for part in parts], axis=1)
        both = split_three(0.5 * jnp.concatenate([top, bottom], axis=0))
        dst[...] = join_three(
            lax.dot_general(both, pairs[...], (((1,), (1,)), ((), ())), preferred_element_type=jnp.float32)
        )

    def denominators():
        for copy in get_energies:
            copy.wait()
        occ = occ_index[...]
        picked = jnp.zeros(occ.shape, jnp.float32)
        for i in range(eps_occ.shape[0]):
            picked = jnp.where(occ == i, eps_occ[i], picked)
        energy = jnp.broadcast_to(picked[0:1] + picked[1:2], (16, occ.shape[1]))
        firsts = jnp.maximum(pairs[...].astype(jnp.float32), 0.0).astype(jnp.bfloat16)
        occ_row = join_three(jnp.dot(split_three(energy), firsts, preferred_element_type=jnp.float32))[0:1]
        table = split_three(jnp.broadcast_to(eps_vir[...], (16, eps_vir.shape[1])))
        orbitals = lax.broadcasted_iota(jnp.int32, (eps_vir.shape[1], 256), 0)
        for i in range(3):
            windows[i].wait()
            found = window[i]
            counts = jnp.where(orbitals == found[0:1], 1.0, 0.0) + jnp.where(orbitals == found[1:2], 1.0, 0.0)
            vir = join_three(jnp.dot(table, counts.astype(jnp.bfloat16), preferred_element_type=jnp.float32))
            vir = pltpu.roll(vir, lax.rem(256 - shifts[i], 256), 1)[0:1, 0:128]
            vir = jnp.broadcast_to(vir, (128, 128)).T
            vir = jnp.where(half, vir[:48], vir[48:96])
            for k in range(n):
                value = vir - occ_row[:, 128 * k : 128 * k + 128]
                if i < 2:
                    den1[i, 48 * k : 48 * k + 48, :] = value
                else:
                    den2[48 * k : 48 * k + 48, :] = value

    get_partner.wait()
    map_pairs()
    differences(amplitudes, own, get_amplitudes)
    get_mask.wait()
    pl.semaphore_wait(barrier, len(peers))

    gather_z = [None] * n
    gather_y = [[] for _ in range(n)]

    def spread_y(k, src, dst):
        for d in (2, 1, 3):
            gather_y[k].append(send(src, dst, at(y_=wrap(y + d, 4))))

    def start_gather(k):
        row, rows = CHUNKS[k]
        gat = bufs[k][0]
        mine = own.at[pl.ds(row, rows)]
        gather_z[k] = [send(mine, gat.at[y, d], at(zl_=wrap(zl + d, 4))) for d in (3, 1, 2)]
        gat[y, 0] = own[row : row + rows]
        if k not in LATE:
            spread_y(k, mine, gat.at[y, 0])

    def forward(k):
        gat = bufs[k][0]
        if k in LATE:
            for copy in gather_z[k]:
                copy.wait_recv()
            spread_y(k, gat.at[y], gat.at[y])
        else:
            for copy, d in zip(gather_z[k][1:] + gather_z[k][:1], (1, 2, 3)):
                copy.wait_recv()
                spread_y(k, gat.at[y, d], gat.at[y, d])

    def split_tile(t):
        for load in loads[t]:
            load.wait()
        pieces = []
        for p, first in enumerate(starts(t)):
            cut = min(48, W * (first // W + 1) - first)
            pieces.append((48 * p, cut, first // W))
            if cut < 48:
                pieces.append((48 * p + cut, 48 - cut, first // W + 1))

        def body(j, carry):
            cols = pl.ds(pl.multiple_of(j * W, W), W)
            for at_row, count, tile in pieces:
                v = stage[t, at_row : at_row + count, cols] * mask[tile, j].astype(jnp.float32)
                h = v.astype(jnp.bfloat16)
                rows = slice(192 * t + at_row, 192 * t + at_row + count)
                hi[rows, cols] = h
                lo[rows, cols] = (v - h.astype(jnp.float32)).astype(jnp.bfloat16)
            return carry

        lax.fori_loop(0, 6, body, 0)

    def turn_out(first, last):
        def body(t, carry):
            q = t % 4
            lanes = pl.ds(pl.multiple_of((t // 4) * W, W), W)
            cols = pl.ds(pl.multiple_of(q * 384, 384), 384)
            for src, dst in ((hi, hi_t), (lo, lo_t)):
                turned = src[lanes, cols].T
                for p in range(4):
                    for h in range(2):
                        rows = pl.ds(pl.multiple_of(768 * h + 192 * q + 48 * p, 16), 48)
                        dst[rows, lanes] = turned[96 * p + 48 * h : 96 * p + 48 * h + 48]
            return carry

        lax.fori_loop(first, last, body, 0)

    def turn_back(first, last):
        def body(t, carry):
            rows = pl.ds(pl.multiple_of((t // 6) * W, W), W)
            cols = pl.ds(pl.multiple_of((t % 6) * W, W), W)
            hi[cols, rows] = hi_t[rows, cols].T
            lo[cols, rows] = lo_t[rows, cols].T
            return carry

        lax.fori_loop(first, last, body, 0)

    def fill_left(slot, slab):
        for i in range(2):
            turned = jnp.concatenate([slab(8 * i + p) for p in range(8)], axis=0).T
            high = turned.astype(jnp.bfloat16)
            low = (turned - high.astype(jnp.float32)).astype(jnp.bfloat16)
            lanes = slice(384 * i, 384 * i + 384)
            for part in range(2):
                left[slot, part, 0:64, lanes] = high[64 * part : 64 * part + 64]
                left[slot, part, 64:128, lanes] = low[64 * part : 64 * part + 64]

    def product(slot, high, low, i):
        parts = []
        for part in range(2):
            lanes = pl.ds(pl.multiple_of(768 * part + 384 * i, 128), 384)
            both = jnp.dot(left[slot, 0], high[0:768, lanes], preferred_element_type=jnp.float32)
            both = both + jnp.dot(left[slot, 1], high[768:1536, lanes], preferred_element_type=jnp.float32)
            rest_ = jnp.dot(left[slot, 0, 0:64], low[0:768, lanes], preferred_element_type=jnp.float32)
            rest_ = rest_ + jnp.dot(left[slot, 1, 0:64], low[768:1536, lanes], preferred_element_type=jnp.float32)
            parts.append(both[0:64] + (both[64:128] + rest_))
        return jnp.concatenate(parts, axis=0).T

    core_copies = [None] * n

    def first_product(k):
        gat, par, corr = bufs[k][0], bufs[k][1], bufs[k][2]
        for copy in gather_y[k]:
            copy.wait_recv()
        fill_left(k, lambda b: gat[b // 4, wrap(zl - b % 4 + 4, 4)])
        base = take(2)

        def core_copy(i):
            return describe(base + i, par.at[1 - c, i], corr.at[i], at(c_=1 - c))

        def body(i, carry):
            packed = product(k, hi_t, lo_t, i)
            for p in range(8):
                par[p % 2, i, p // 2] = packed[48 * p : 48 * p + 48]
            core_copy(i).start()
            return carry

        lax.fori_loop(0, 2, body, 0)
        core_copies[k] = [core_copy(i) for i in range(2)]
        sent.extend(core_copies[k])

    x_copies = [None] * n

    def reduce_x(k):
        par, corr, xsum, xrecv = bufs[k][1], bufs[k][2], bufs[k][3], bufs[k][4]
        for copy in core_copies[k]:
            copy.wait_recv()
        x_copies[k] = []
        for d in (2, 1, 3, 0):
            xd = wrap(x + d, 4)
            for h in range(2):
                xsum[xd, h] = par[c, h, xd] + corr[h, xd]
            if d:
                x_copies[k].append(send(xsum.at[xd], xrecv.at[d - 1], at(x_=xd)))

    h_copies = [None] * n

    def reduce_h(k):
        xsum, xrecv, hsum, hrecv = bufs[k][3], bufs[k][4], bufs[k][5], bufs[k][6]
        for copy in x_copies[k]:
            copy.wait_recv()
        for h in range(2):
            hsum[h] = (xsum[x, h] + xrecv[1, h]) + (xrecv[0, h] + xrecv[2, h])
        h_copies[k] = send(hsum, hrecv, at(zh_=1 - zh))

    ux_copies = [None] * n
    uc_copies = [None] * n

    def forward_core(k, first, count):
        ug = bufs[k][7]
        piece = ug.at[c, pl.ds(first, count)]
        uc_copies[k].append(send(piece, piece, at(c_=1 - c)))

    def update_one(k):
        row, rows = CHUNKS[k]
        hsum, hrecv, ug = bufs[k][5], bufs[k][6], bufs[k][7]
        h_copies[k].wait_recv()
        here = slice(row, row + rows)
        both = []
        for h in range(2):
            other = jnp.where(zh == h, oth1[here, :], oth1_peer[here, :])
            value = (other + (hsum[h] + hrecv[h])) / den1[h, here, :]
            ug[c, 0, h] = value
            both.append(value)
        ux_copies[k] = []
        uc_copies[k] = []
        for d in (2, 1, 3):
            ux_copies[k].append(send(ug.at[c, 0], ug.at[c, d], at(x_=wrap(x + d, 4))))
        forward_core(k, 0, 1)
        new1[here, :] = jnp.where(zh == 0, both[0], both[1])

    def pass_core(k):
        for copy in ux_copies[k]:
            copy.wait_recv()
        forward_core(k, 1, 3)

    y_copies = [None] * n

    def second_product(k):
        ug, par, yrecv = bufs[k][7], bufs[k][8], bufs[k][9]
        for copy in uc_copies[k]:
            copy.wait_recv()
        fill_left(3 + k, lambda b: ug[b % 2, wrap(x - (b // 2) % 4 + 4, 4), b // 8])
        base = take(3)

        def y_copy(yd, d):
            return describe(base + d - 1, par.at[yd], yrecv.at[d - 1], at(y_=yd))

        def body(i, carry):
            packed = product(3 + k, hi, lo, i)
            for p in range(8):
                par[2 * i + p // 4, p % 4] = packed[48 * p : 48 * p + 48]
            for e in range(2):
                yd = 2 * i + e
                d = lax.rem(yd - y + 4, 4)

                @pl.when(d > 0)
                def _():
                    y_copy(yd, d).start()

            return carry

        lax.fori_loop(0, 2, body, 0)
        y_copies[k] = [y_copy(wrap(y + d, 4), d) for d in (1, 2, 3)]
        sent.extend(y_copies[k])

    l_copies = [None] * n

    def reduce_l(k):
        par, yrecv, ysum, lrecv = bufs[k][8], bufs[k][9], bufs[k][10], bufs[k][11]
        for copy in y_copies[k]:
            copy.wait_recv()
        l_copies[k] = []
        for d in (2, 1, 3, 0):
            ld = wrap(zl + d, 4)
            ysum[ld] = (par[y, ld] + yrecv[0, ld]) + (yrecv[1, ld] + yrecv[2, ld])
            if d:
                l_copies[k].append(send(ysum.at[ld], lrecv.at[d - 1], at(zl_=ld)))

    def update_two(k):
        row, rows = CHUNKS[k]
        ysum, lrecv = bufs[k][10], bufs[k][11]
        for copy in l_copies[k]:
            copy.wait_recv()
        here = slice(row, row + rows)
        ladder = (ysum[zl] + lrecv[0]) + (lrecv[1] + lrecv[2])
        new2[here, :] = (oth2[here, :] + ladder) / den2[here, :]

    start_gather(0)
    start_gather(1)
    split_tile(0)
    split_tile(1)
    split_tile(2)
    split_tile(3)
    forward(0)
    start_gather(2)
    split_tile(4)
    split_tile(5)
    forward(1)
    split_tile(6)
    split_tile(7)
    turn_out(0, 24)
    forward(2)
    differences(other_first, oth1, get_first)
    other_copy = send(oth1, oth1_peer, at(zh_=1 - zh))
    first_product(0)
    denominators()
    reduce_x(0)
    first_product(1)
    reduce_h(0)
    reduce_x(1)
    first_product(2)
    turn_back(0, 18)
    differences(other_second, oth2, get_second)
    other_copy.wait_recv()
    update_one(0)
    reduce_h(1)
    reduce_x(2)
    turn_back(18, 36)
    pass_core(0)
    update_one(1)
    reduce_h(2)
    second_product(0)
    pass_core(1)
    update_one(2)
    second_product(1)
    pass_core(2)
    reduce_l(0)
    expand(new1, result1)
    second_product(2)
    reduce_l(1)
    update_two(0)
    reduce_l(2)
    update_two(1)
    update_two(2)
    expand(new2, result2)
    for copy in sent:
        copy.wait_send()


def per_device(
    integrals,
    tile_mask,
    amplitudes,
    other_first,
    other_second,
    vir_index,
    occ_index,
    partner,
    eps_vir,
    eps_occ,
):
    f32, bf16 = jnp.float32, jnp.bfloat16
    side = integrals.shape[0]
    packed = (144, 128)
    scratch = [pltpu.VMEM((8, 192, side), f32)]
    scratch += [pltpu.VMEM((side, side), bf16)] * 4
    scratch += [pltpu.VMEM((6, 2, 128, side // 2), bf16)]
    scratch += [pltpu.VMEM(packed, f32)] * 4
    scratch += [pltpu.VMEM((2,) + packed, f32)]
    scratch += [pltpu.VMEM(packed, f32)] * 3
    scratch += [pltpu.VMEM((384, 384), bf16), pltpu.VMEM((3, 2, 256), jnp.int32)]
    scratch += [pltpu.SMEM(tile_mask.shape, jnp.int32)] + [pltpu.VMEM(amplitudes.shape, f32)] * 3
    scratch += [pltpu.VMEM(occ_index.shape, jnp.int32), pltpu.VMEM((1,) + partner.shape, jnp.int32)]
    scratch += [pltpu.VMEM((1,) + eps_vir.shape, f32), pltpu.SMEM(eps_occ.shape, f32)]
    for _, rows in CHUNKS:
        for lead in (
            (4, 4), (2, 2, 4), (2, 4), (4, 2), (3, 2), (2,), (2,), (2, 4, 2), (4, 4), (3, 4), (4,), (3,)
        ):
            scratch.append(pltpu.VMEM(lead + (rows, 128), f32))
    scratch += [
        pltpu.SemaphoreType.DMA((8, 4)),
        pltpu.SemaphoreType.DMA((3,)),
        pltpu.SemaphoreType.DMA((10,)),
        pltpu.SemaphoreType.DMA((N_SEMS,)),
        pltpu.SemaphoreType.DMA((N_SEMS,)),
    ]
    hbm = pl.BlockSpec(memory_space=pl.ANY)
    shapes = [jax.ShapeDtypeStruct(amplitudes.shape, f32)] * 2
    return pl.pallas_call(
        ladder_kernel,
        out_shape=shapes,
        in_specs=[hbm] * 10,
        out_specs=[pl.BlockSpec(memory_space=pltpu.VMEM)] * 2,
        scratch_shapes=scratch,
        compiler_params=pltpu.CompilerParams(
            collective_id=0, has_side_effects=True, vmem_limit_bytes=53 * 1024 * 1024
        ),
        name="ladders",
    )(
        integrals, tile_mask, amplitudes, other_first, other_second, vir_index, occ_index, partner, eps_vir, eps_occ
    )


def solution(mesh):
    return jax.shard_map(
        per_device,
        mesh=mesh,
        in_specs=(
            P("res", "con"),
            P("res", "con"),
            P(("con", "res"), None),
            P(("res", "con"), None),
            P(("con", "res"), None),
            P(),
            P(),
            P(),
            P(),
            P(),
        ),
        out_specs=(P(("res", "con"), None), P(("con", "res"), None)),
        check_vma=False,
    )
```

```python
import jax
import jax.numpy as jnp
from jax import lax
from jax.experimental import pallas as pl
from jax.experimental.pallas import tpu as pltpu
from jax.sharding import PartitionSpec as P

W = 256
MESH = pl.DeviceIdType.MESH

N_X, N_C, N_H, N_Y, N_L = 4, 2, 2, 4, 4
CHUNKS = ((0, 48), (48, 48), (96, 48))
N_SEMS = 128
LATE = (1, 2)


def split_three(v):
    one = v.astype(jnp.bfloat16)
    v = v - one.astype(jnp.float32)
    two = v.astype(jnp.bfloat16)
    three = (v - two.astype(jnp.float32)).astype(jnp.bfloat16)
    return jnp.concatenate([one, two, three], axis=0)


def join_three(v):
    n = v.shape[0] // 3
    return (v[2 * n :] + v[n : 2 * n]) + v[:n]


def ladder_kernel(
    integrals, mask_in, amplitudes_in, first_in, second_in, vir_index, occ_in, partner_in, vir_in, eps_occ_in,
    result1, result2, stage, hi, lo, hi_t, lo_t, left, own, oth1, oth1_peer, oth2, den1, den2, new1,
    new2, pairs, window, mask, amplitudes, other_first, other_second, occ_index, partner, eps_vir, eps_occ, *rest
):
    n = len(CHUNKS)
    per = 12
    bufs = [rest[per * k : per * k + per] for k in range(n)]
    stage_sem, window_sem, small_sem, ssem, rsem = rest[per * n :]
    con = lax.axis_index("con")
    res = lax.axis_index("res")
    zh, x, c = con // 8, (con // 2) % 4, con % 2
    y, zl = res // 4, res % 4

    def wrap(v, m):
        return lax.rem(v + m, m)

    def at(zh_=None, x_=None, c_=None, y_=None, zl_=None):
        zh_ = zh if zh_ is None else zh_
        x_ = x if x_ is None else x_
        c_ = c if c_ is None else c_
        y_ = y if y_ is None else y_
        zl_ = zl if zl_ is None else zl_
        return (zh_ * 8 + x_ * 2 + c_, y_ * 4 + zl_)

    used = [0]
    sent = []

    def take(count):
        first = used[0]
        used[0] += count
        return first

    def describe(index, src, dst, device):
        return pltpu.make_async_remote_copy(
            src_ref=src, dst_ref=dst, send_sem=ssem.at[index], recv_sem=rsem.at[index],
            device_id=device, device_id_type=MESH,
        )

    def send(src, dst, device):
        copy = describe(take(1), src, dst, device)
        copy.start()
        sent.append(copy)
        return copy

    peers = (
        [at(zl_=wrap(zl + d, 4)) for d in (1, 2, 3)]
        + [at(y_=wrap(y + d, 4)) for d in (1, 2, 3)]
        + [at(x_=wrap(x + d, 4)) for d in (1, 2, 3)]
        + [at(c_=1 - c), at(zh_=1 - zh)]
    )
    barrier = pltpu.get_barrier_semaphore()
    for peer in peers:
        pl.semaphore_signal(barrier, inc=1, device_id=peer, device_id_type=MESH)

    def bring(i, src, dst):
        copy = pltpu.make_async_copy(src, dst, small_sem.at[i])
        copy.start()
        return copy

    get_partner = bring(0, partner_in, partner.at[0])
    get_amplitudes = bring(1, amplitudes_in, amplitudes)
    get_mask = bring(2, mask_in, mask)
    def starts(t):
        return [96 * (4 * (t % 4) + p) + 48 * (t // 4) for p in range(4)]

    loads = [
        [
            pltpu.make_async_copy(
                integrals.at[pl.ds(first, 48)], stage.at[t, pl.ds(48 * p, 48)], stage_sem.at[t, p]
            )
            for p, first in enumerate(starts(t))
        ]
        for t in range(8)
    ]
    for group in loads:
        for load in group:
            load.start()
    get_first = bring(3, first_in, other_first)
    get_second = bring(4, second_in, other_second)
    get_energies = [
        bring(5, occ_in, occ_index), bring(6, vir_in, eps_vir.at[0]), bring(7, eps_occ_in, eps_occ)
    ]
    blocks = (res * 16 + con % 8, res * 16 + 8 + con % 8, con * 16 + res)
    shifts, windows = [], []
    for i, block in enumerate(blocks):
        first = lax.min(block * 96 // 128 * 128, vir_index.shape[1] - 256)
        first = pl.multiple_of(first, 128)
        shifts.append(block * 96 - first)
        windows.append(
            pltpu.make_async_copy(vir_index.at[:, pl.ds(first, 256)], window.at[i], window_sem.at[i])
        )
        windows[i].start()

    half = lax.broadcasted_iota(jnp.int32, (48, 128), 1) < 64

    def map_pairs():
        size = partner.shape[1]
        row = partner[...].astype(jnp.float32)
        col = jnp.broadcast_to(row, (128, size)).T
        col = jnp.concatenate([col] * (size // 128), axis=1)
        down = lax.broadcasted_iota(jnp.int32, (size, size), 0).astype(jnp.float32)
        across = lax.broadcasted_iota(jnp.int32, (size, size), 1)
        wide = across.astype(jnp.float32)
        before = (wide < jnp.minimum(down, col)) & (wide < jnp.broadcast_to(row, (size, size)))
        before = jnp.where(before, 1.0, 0.0).astype(jnp.bfloat16)
        couple = jnp.dot(before, jnp.ones((size, size), jnp.bfloat16), preferred_element_type=jnp.float32)
        place = (64 * (across // 128) + across % 64).astype(jnp.float32)
        sign = jnp.where(down < col, 1.0, -1.0)
        pairs[...] = jnp.where(couple == place, sign, 0.0).astype(jnp.bfloat16)

    def differences(src, dst, copy):
        copy.wait()
        wide = join_three(jnp.dot(split_three(src[...]), pairs[...], preferred_element_type=jnp.float32))
        for k in range(n):
            part = wide[:, 128 * k : 128 * k + 128]
            dst[48 * k : 48 * k + 48, :] = jnp.where(half, part[:48], part[48:])

    def expand(src, dst):
        parts = [src[48 * k : 48 * k + 48, :] for k in range(n)]
        top = jnp.concatenate([jnp.where(half, part, 0.0) for part in parts], axis=1)
        bottom = jnp.concatenate([jnp.where(half, 0.0, part) for part in parts], axis=1)
        both = split_three(0.5 * jnp.concatenate([top, bottom], axis=0))
        dst[...] = join_three(
            lax.dot_general(both, pairs[...], (((1,), (1,)), ((), ())), preferred_element_type=jnp.float32)
        )

    def denominators():
        for copy in get_energies:
            copy.wait()
        occ = occ_index[...]
        picked = jnp.zeros(occ.shape, jnp.float32)
        for i in range(eps_occ.shape[0]):
            picked = jnp.where(occ == i, eps_occ[i], picked)
        energy = jnp.broadcast_to(picked[0:1] + picked[1:2], (16, occ.shape[1]))
        firsts = jnp.maximum(pairs[...].astype(jnp.float32), 0.0).astype(jnp.bfloat16)
        occ_row = join_three(jnp.dot(split_three(energy), firsts, preferred_element_type=jnp.float32))[0:1]
        table = split_three(jnp.broadcast_to(eps_vir[...], (16, eps_vir.shape[1])))
        orbitals = lax.broadcasted_iota(jnp.int32, (eps_vir.shape[1], 256), 0)
        for i in range(3):
            windows[i].wait()
            found = window[i]
            counts = jnp.where(orbitals == found[0:1], 1.0, 0.0) + jnp.where(orbitals == found[1:2], 1.0, 0.0)
            vir = join_three(jnp.dot(table, counts.astype(jnp.bfloat16), preferred_element_type=jnp.float32))
            vir = pltpu.roll(vir, lax.rem(256 - shifts[i], 256), 1)[0:1, 0:128]
            vir = jnp.broadcast_to(vir, (128, 128)).T
            vir = jnp.where(half, vir[:48], vir[48:96])
            for k in range(n):
                value = vir - occ_row[:, 128 * k : 128 * k + 128]
                if i < 2:
                    den1[i, 48 * k : 48 * k + 48, :] = value
                else:
                    den2[48 * k : 48 * k + 48, :] = value

    get_partner.wait()
    map_pairs()
    differences(amplitudes, own, get_amplitudes)
    get_mask.wait()
    pl.semaphore_wait(barrier, len(peers))

    gather_z = [None] * n
    gather_y = [[] for _ in range(n)]

    def spread_y(k, src, dst):
        for d in (2, 1, 3):
            gather_y[k].append(send(src, dst, at(y_=wrap(y + d, 4))))

    def start_gather(k):
        row, rows = CHUNKS[k]
        gat = bufs[k][0]
        mine = own.at[pl.ds(row, rows)]
        gather_z[k] = [send(mine, gat.at[y, d], at(zl_=wrap(zl + d, 4))) for d in (3, 1, 2)]
        gat[y, 0] = own[row : row + rows]
        if k not in LATE:
            spread_y(k, mine, gat.at[y, 0])

    def forward(k):
        gat = bufs[k][0]
        if k in LATE:
            for copy in gather_z[k]:
                copy.wait_recv()
            spread_y(k, gat.at[y], gat.at[y])
        else:
            for copy, d in zip(gather_z[k][1:] + gather_z[k][:1], (1, 2, 3)):
                copy.wait_recv()
                spread_y(k, gat.at[y, d], gat.at[y, d])

    def split_tile(t):
        for load in loads[t]:
            load.wait()
        pieces = []
        for p, first in enumerate(starts(t)):
            cut = min(48, W * (first // W + 1) - first)
            pieces.append((48 * p, cut, first // W))
            if cut < 48:
                pieces.append((48 * p + cut, 48 - cut, first // W + 1))

        def body(j, carry):
            cols = pl.ds(pl.multiple_of(j * W, W), W)
            for at_row, count, tile in pieces:
                v = stage[t, at_row : at_row + count, cols] * mask[tile, j].astype(jnp.float32)
                h = v.astype(jnp.bfloat16)
                rows = slice(192 * t + at_row, 192 * t + at_row + count)
                hi[rows, cols] = h
                lo[rows, cols] = (v - h.astype(jnp.float32)).astype(jnp.bfloat16)
            return carry

        lax.fori_loop(0, 6, body, 0)

    def turn_out(first, last):
        def body(t, carry):
            q = t % 4
            lanes = pl.ds(pl.multiple_of((t // 4) * W, W), W)
            cols = pl.ds(pl.multiple_of(q * 384, 384), 384)
            for src, dst in ((hi, hi_t), (lo, lo_t)):
                turned = src[lanes, cols].T
                for p in range(4):
                    for h in range(2):
                        rows = pl.ds(pl.multiple_of(768 * h + 192 * q + 48 * p, 16), 48)
                        dst[rows, lanes] = turned[96 * p + 48 * h : 96 * p + 48 * h + 48]
            return carry

        lax.fori_loop(first, last, body, 0)

    def turn_back(first, last):
        def body(t, carry):
            rows = pl.ds(pl.multiple_of((t // 6) * W, W), W)
            cols = pl.ds(pl.multiple_of((t % 6) * W, W), W)
            hi[cols, rows] = hi_t[rows, cols].T
            lo[cols, rows] = lo_t[rows, cols].T
            return carry

        lax.fori_loop(first, last, body, 0)

    def fill_left(slot, slab):
        for i in range(2):
            turned = jnp.concatenate([slab(8 * i + p) for p in range(8)], axis=0).T
            high = turned.astype(jnp.bfloat16)
            low = (turned - high.astype(jnp.float32)).astype(jnp.bfloat16)
            lanes = slice(384 * i, 384 * i + 384)
            for part in range(2):
                left[slot, part, 0:64, lanes] = high[64 * part : 64 * part + 64]
                left[slot, part, 64:128, lanes] = low[64 * part : 64 * part + 64]

    def product(slot, high, low, i):
        parts = []
        for part in range(2):
            lanes = pl.ds(pl.multiple_of(768 * part + 384 * i, 128), 384)
            both = jnp.dot(left[slot, 0], high[0:768, lanes], preferred_element_type=jnp.float32)
            both = both + jnp.dot(left[slot, 1], high[768:1536, lanes], preferred_element_type=jnp.float32)
            rest_ = jnp.dot(left[slot, 0, 0:64], low[0:768, lanes], preferred_element_type=jnp.float32)
            rest_ = rest_ + jnp.dot(left[slot, 1, 0:64], low[768:1536, lanes], preferred_element_type=jnp.float32)
            parts.append(both[0:64] + (both[64:128] + rest_))
        return jnp.concatenate(parts, axis=0).T

    core_copies = [None] * n

    def first_product(k):
        gat, par, corr = bufs[k][0], bufs[k][1], bufs[k][2]
        for copy in gather_y[k]:
            copy.wait_recv()
        fill_left(k, lambda b: gat[b // 4, wrap(zl - b % 4 + 4, 4)])
        base = take(2)

        def core_copy(i):
            return describe(base + i, par.at[1 - c, i], corr.at[i], at(c_=1 - c))

        def body(i, carry):
            packed = product(k, hi_t, lo_t, i)
            for p in range(8):
                par[p % 2, i, p // 2] = packed[48 * p : 48 * p + 48]
            core_copy(i).start()
            return carry

        lax.fori_loop(0, 2, body, 0)
        core_copies[k] = [core_copy(i) for i in range(2)]
        sent.extend(core_copies[k])

    x_copies = [None] * n

    def reduce_x(k):
        par, corr, xsum, xrecv = bufs[k][1], bufs[k][2], bufs[k][3], bufs[k][4]
        for copy in core_copies[k]:
            copy.wait_recv()
        x_copies[k] = []
        for d in (2, 1, 3, 0):
            xd = wrap(x + d, 4)
            for h in range(2):
                xsum[xd, h] = par[c, h, xd] + corr[h, xd]
            if d:
                x_copies[k].append(send(xsum.at[xd], xrecv.at[d - 1], at(x_=xd)))

    h_copies = [None] * n

    def reduce_h(k):
        xsum, xrecv, hsum, hrecv = bufs[k][3], bufs[k][4], bufs[k][5], bufs[k][6]
        for copy in x_copies[k]:
            copy.wait_recv()
        for h in range(2):
            hsum[h] = (xsum[x, h] + xrecv[1, h]) + (xrecv[0, h] + xrecv[2, h])
        h_copies[k] = send(hsum, hrecv, at(zh_=1 - zh))

    ux_copies = [None] * n
    uc_copies = [None] * n

    def forward_core(k, first, count):
        ug = bufs[k][7]
        piece = ug.at[c, pl.ds(first, count)]
        uc_copies[k].append(send(piece, piece, at(c_=1 - c)))

    def update_one(k):
        row, rows = CHUNKS[k]
        hsum, hrecv, ug = bufs[k][5], bufs[k][6], bufs[k][7]
        h_copies[k].wait_recv()
        here = slice(row, row + rows)
        both = []
        for h in range(2):
            other = jnp.where(zh == h, oth1[here, :], oth1_peer[here, :])
            value = (other + (hsum[h] + hrecv[h])) / den1[h, here, :]
            ug[c, 0, h] = value
            both.append(value)
        ux_copies[k] = []
        uc_copies[k] = []
        for d in (2, 1, 3):
            ux_copies[k].append(send(ug.at[c, 0], ug.at[c, d], at(x_=wrap(x + d, 4))))
        forward_core(k, 0, 1)
        new1[here, :] = jnp.where(zh == 0, both[0], both[1])

    def pass_core(k):
        for copy in ux_copies[k]:
            copy.wait_recv()
        forward_core(k, 1, 3)

    y_copies = [None] * n

    def second_product(k):
        ug, par, yrecv = bufs[k][7], bufs[k][8], bufs[k][9]
        for copy in uc_copies[k]:
            copy.wait_recv()
        fill_left(3 + k, lambda b: ug[b % 2, wrap(x - (b // 2) % 4 + 4, 4), b // 8])
        base = take(3)

        def y_copy(yd, d):
            return describe(base + d - 1, par.at[yd], yrecv.at[d - 1], at(y_=yd))

        def body(i, carry):
            packed = product(3 + k, hi, lo, i)
            for p in range(8):
                par[2 * i + p // 4, p % 4] = packed[48 * p : 48 * p + 48]
            for e in range(2):
                yd = 2 * i + e
                d = lax.rem(yd - y + 4, 4)

                @pl.when(d > 0)
                def _():
                    y_copy(yd, d).start()

            return carry

        lax.fori_loop(0, 2, body, 0)
        y_copies[k] = [y_copy(wrap(y + d, 4), d) for d in (1, 2, 3)]
        sent.extend(y_copies[k])

    l_copies = [None] * n

    def reduce_l(k):
        par, yrecv, ysum, lrecv = bufs[k][8], bufs[k][9], bufs[k][10], bufs[k][11]
        for copy in y_copies[k]:
            copy.wait_recv()
        l_copies[k] = []
        for d in (2, 1, 3, 0):
            ld = wrap(zl + d, 4)
            ysum[ld] = (par[y, ld] + yrecv[0, ld]) + (yrecv[1, ld] + yrecv[2, ld])
            if d:
                l_copies[k].append(send(ysum.at[ld], lrecv.at[d - 1], at(zl_=ld)))

    def update_two(k):
        row, rows = CHUNKS[k]
        ysum, lrecv = bufs[k][10], bufs[k][11]
        for copy in l_copies[k]:
            copy.wait_recv()
        here = slice(row, row + rows)
        ladder = (ysum[zl] + lrecv[0]) + (lrecv[1] + lrecv[2])
        new2[here, :] = (oth2[here, :] + ladder) / den2[here, :]

    start_gather(0)
    start_gather(1)
    split_tile(0)
    split_tile(1)
    split_tile(2)
    split_tile(3)
    forward(0)
    start_gather(2)
    split_tile(4)
    split_tile(5)
    forward(1)
    split_tile(6)
    split_tile(7)
    turn_out(0, 24)
    forward(2)
    differences(other_first, oth1, get_first)
    other_copy = send(oth1, oth1_peer, at(zh_=1 - zh))
    first_product(0)
    denominators()
    reduce_x(0)
    first_product(1)
    reduce_h(0)
    reduce_x(1)
    first_product(2)
    turn_back(0, 18)
    differences(other_second, oth2, get_second)
    other_copy.wait_recv()
    update_one(0)
    reduce_h(1)
    reduce_x(2)
    turn_back(18, 36)
    pass_core(0)
    update_one(1)
    reduce_h(2)
    second_product(0)
    pass_core(1)
    update_one(2)
    second_product(1)
    pass_core(2)
    reduce_l(0)
    expand(new1, result1)
    second_product(2)
    reduce_l(1)
    update_two(0)
    reduce_l(2)
    update_two(1)
    update_two(2)
    expand(new2, result2)
    for copy in sent:
        copy.wait_send()


def per_device(
    integrals,
    tile_mask,
    amplitudes,
    other_first,
    other_second,
    vir_index,
    occ_index,
    partner,
    eps_vir,
    eps_occ,
):
    f32, bf16 = jnp.float32, jnp.bfloat16
    side = integrals.shape[0]
    packed = (144, 128)
    scratch = [pltpu.VMEM((8, 192, side), f32)]
    scratch += [pltpu.VMEM((side, side), bf16)] * 4
    scratch += [pltpu.VMEM((6, 2, 128, side // 2), bf16)]
    scratch += [pltpu.VMEM(packed, f32)] * 4
    scratch += [pltpu.VMEM((2,) + packed, f32)]
    scratch += [pltpu.VMEM(packed, f32)] * 3
    scratch += [pltpu.VMEM((384, 384), bf16), pltpu.VMEM((3, 2, 256), jnp.int32)]
    scratch += [pltpu.SMEM(tile_mask.shape, jnp.int32)] + [pltpu.VMEM(amplitudes.shape, f32)] * 3
    scratch += [pltpu.VMEM(occ_index.shape, jnp.int32), pltpu.VMEM((1,) + partner.shape, jnp.int32)]
    scratch += [pltpu.VMEM((1,) + eps_vir.shape, f32), pltpu.SMEM(eps_occ.shape, f32)]
    for _, rows in CHUNKS:
        for lead in (
            (4, 4), (2, 2, 4), (2, 4), (4, 2), (3, 2), (2,), (2,), (2, 4, 2), (4, 4), (3, 4), (4,), (3,)
        ):
            scratch.append(pltpu.VMEM(lead + (rows, 128), f32))
    scratch += [
        pltpu.SemaphoreType.DMA((8, 4)),
        pltpu.SemaphoreType.DMA((3,)),
        pltpu.SemaphoreType.DMA((10,)),
        pltpu.SemaphoreType.DMA((N_SEMS,)),
        pltpu.SemaphoreType.DMA((N_SEMS,)),
    ]
    hbm = pl.BlockSpec(memory_space=pl.ANY)
    shapes = [jax.ShapeDtypeStruct(amplitudes.shape, f32)] * 2
    return pl.pallas_call(
        ladder_kernel,
        out_shape=shapes,
        in_specs=[hbm] * 10,
        out_specs=[pl.BlockSpec(memory_space=pltpu.VMEM)] * 2,
        scratch_shapes=scratch,
        compiler_params=pltpu.CompilerParams(
            collective_id=0, has_side_effects=True, vmem_limit_bytes=53 * 1024 * 1024
        ),
        name="ladders",
    )(
        *(
            pltpu.with_memory_space_constraint(value, pltpu.HBM)
            for value in (
                integrals, tile_mask, amplitudes, other_first, other_second,
                vir_index, occ_index, partner, eps_vir, eps_occ,
            )
        )
    )


def solution(mesh):
    return jax.shard_map(
        per_device,
        mesh=mesh,
        in_specs=(
            P("res", "con"),
            P("res", "con"),
            P(("con", "res"), None),
            P(("res", "con"), None),
            P(("con", "res"), None),
            P(),
            P(),
            P(),
            P(),
            P(),
        ),
        out_specs=(P(("res", "con"), None), P(("con", "res"), None)),
        check_vma=False,
    )
```

```python
import jax
import jax.numpy as jnp
from jax import lax
from jax.experimental import pallas as pl
from jax.experimental.pallas import tpu as pltpu
from jax.sharding import PartitionSpec as P

W = 256
MESH = pl.DeviceIdType.MESH

N_X, N_C, N_H, N_Y, N_L = 4, 2, 2, 4, 4
CHUNKS = ((0, 48), (48, 48), (96, 48))
N_SEMS = 128
LATE = (1, 2)


def split_three(v):
    one = v.astype(jnp.bfloat16)
    v = v - one.astype(jnp.float32)
    two = v.astype(jnp.bfloat16)
    three = (v - two.astype(jnp.float32)).astype(jnp.bfloat16)
    return jnp.concatenate([one, two, three], axis=0)


def join_three(v):
    n = v.shape[0] // 3
    return (v[2 * n :] + v[n : 2 * n]) + v[:n]


def ladder_kernel(
    integrals, mask_in, amplitudes_in, first_in, second_in, vir_index, occ_in, partner_in, vir_in, eps_occ_in,
    result1, result2, stage, hi, lo, hi_t, lo_t, left, own, oth1, oth1_peer, oth2, den1, den2, new1,
    new2, pairs, window, mask, amplitudes, other_first, other_second, occ_index, partner, eps_vir, eps_occ, *rest
):
    n = len(CHUNKS)
    per = 12
    bufs = [rest[per * k : per * k + per] for k in range(n)]
    stage_sem, window_sem, small_sem, ssem, rsem = rest[per * n :]
    con = lax.axis_index("con")
    res = lax.axis_index("res")
    zh, x, c = con // 8, (con // 2) % 4, con % 2
    y, zl = res // 4, res % 4

    def wrap(v, m):
        return lax.rem(v + m, m)

    def at(zh_=None, x_=None, c_=None, y_=None, zl_=None):
        zh_ = zh if zh_ is None else zh_
        x_ = x if x_ is None else x_
        c_ = c if c_ is None else c_
        y_ = y if y_ is None else y_
        zl_ = zl if zl_ is None else zl_
        return (zh_ * 8 + x_ * 2 + c_, y_ * 4 + zl_)

    used = [0]
    sent = []

    def take(count):
        first = used[0]
        used[0] += count
        return first

    def describe(index, src, dst, device):
        return pltpu.make_async_remote_copy(
            src_ref=src, dst_ref=dst, send_sem=ssem.at[index], recv_sem=rsem.at[index],
            device_id=device, device_id_type=MESH,
        )

    def send(src, dst, device):
        copy = describe(take(1), src, dst, device)
        copy.start()
        sent.append(copy)
        return copy

    peers = (
        [at(zl_=wrap(zl + d, 4)) for d in (1, 2, 3)]
        + [at(y_=wrap(y + d, 4)) for d in (1, 2, 3)]
        + [at(x_=wrap(x + d, 4)) for d in (1, 2, 3)]
        + [at(c_=1 - c), at(zh_=1 - zh)]
    )
    barrier = pltpu.get_barrier_semaphore()
    for peer in peers:
        pl.semaphore_signal(barrier, inc=1, device_id=peer, device_id_type=MESH)

    def bring(i, src, dst):
        copy = pltpu.make_async_copy(src, dst, small_sem.at[i])
        copy.start()
        return copy

    get_partner = bring(0, partner_in, partner.at[0])
    get_amplitudes = bring(1, amplitudes_in, amplitudes)
    get_mask = bring(2, mask_in, mask)
    def starts(t):
        return [96 * (4 * (t % 4) + p) + 48 * (t // 4) for p in range(4)]

    loads = [
        [
            pltpu.make_async_copy(
                integrals.at[pl.ds(first, 48)], stage.at[t, pl.ds(48 * p, 48)], stage_sem.at[t, p]
            )
            for p, first in enumerate(starts(t))
        ]
        for t in range(8)
    ]
    for group in loads:
        for load in group:
            load.start()
    get_first = bring(3, first_in, other_first)
    get_second = bring(4, second_in, other_second)
    get_energies = [
        bring(5, occ_in, occ_index), bring(6, vir_in, eps_vir.at[0]), bring(7, eps_occ_in, eps_occ)
    ]
    blocks = (res * 16 + con % 8, res * 16 + 8 + con % 8, con * 16 + res)
    shifts, windows = [], []
    for i, block in enumerate(blocks):
        first = lax.min(block * 96 // 128 * 128, vir_index.shape[1] - 256)
        first = pl.multiple_of(first, 128)
        shifts.append(block * 96 - first)
        windows.append(
            pltpu.make_async_copy(vir_index.at[:, pl.ds(first, 256)], window.at[i], window_sem.at[i])
        )
        windows[i].start()

    half = lax.broadcasted_iota(jnp.int32, (48, 128), 1) < 64

    def map_pairs():
        size = partner.shape[1]
        row = partner[...].astype(jnp.float32)
        col = jnp.broadcast_to(row, (128, size)).T
        col = jnp.concatenate([col] * (size // 128), axis=1)
        down = lax.broadcasted_iota(jnp.int32, (size, size), 0).astype(jnp.float32)
        across = lax.broadcasted_iota(jnp.int32, (size, size), 1)
        wide = across.astype(jnp.float32)
        before = (wide < jnp.minimum(down, col)) & (wide < jnp.broadcast_to(row, (size, size)))
        before = jnp.where(before, 1.0, 0.0).astype(jnp.bfloat16)
        couple = jnp.dot(before, jnp.ones((size, size), jnp.bfloat16), preferred_element_type=jnp.float32)
        place = (64 * (across // 128) + across % 64).astype(jnp.float32)
        sign = jnp.where(down < col, 1.0, -1.0)
        pairs[...] = jnp.where(couple == place, sign, 0.0).astype(jnp.bfloat16)

    def differences(src, dst, copy):
        copy.wait()
        wide = join_three(jnp.dot(split_three(src[...]), pairs[...], preferred_element_type=jnp.float32))
        for k in range(n):
            part = wide[:, 128 * k : 128 * k + 128]
            dst[48 * k : 48 * k + 48, :] = jnp.where(half, part[:48], part[48:])

    def expand(src, dst, first, last):
        parts = [src[48 * k : 48 * k + 48, :] for k in range(first, last)]
        top = jnp.concatenate([jnp.where(half, part, 0.0) for part in parts], axis=1)
        bottom = jnp.concatenate([jnp.where(half, 0.0, part) for part in parts], axis=1)
        both = split_three(0.5 * jnp.concatenate([top, bottom], axis=0))
        value = join_three(
            lax.dot_general(
                both,
                pairs[:, 128 * first : 128 * last],
                (((1,), (1,)), ((), ())),
                preferred_element_type=jnp.float32,
            )
        )
        dst[...] = value if first == 0 else dst[...] + value

    def denominators():
        for copy in get_energies:
            copy.wait()
        occ = occ_index[...]
        picked = jnp.zeros(occ.shape, jnp.float32)
        for i in range(eps_occ.shape[0]):
            picked = jnp.where(occ == i, eps_occ[i], picked)
        energy = jnp.broadcast_to(picked[0:1] + picked[1:2], (16, occ.shape[1]))
        firsts = jnp.maximum(pairs[...].astype(jnp.float32), 0.0).astype(jnp.bfloat16)
        occ_row = join_three(jnp.dot(split_three(energy), firsts, preferred_element_type=jnp.float32))[0:1]
        table = split_three(jnp.broadcast_to(eps_vir[...], (16, eps_vir.shape[1])))
        orbitals = lax.broadcasted_iota(jnp.int32, (eps_vir.shape[1], 256), 0)
        for i in range(3):
            windows[i].wait()
            found = window[i]
            counts = jnp.where(orbitals == found[0:1], 1.0, 0.0) + jnp.where(orbitals == found[1:2], 1.0, 0.0)
            vir = join_three(jnp.dot(table, counts.astype(jnp.bfloat16), preferred_element_type=jnp.float32))
            vir = pltpu.roll(vir, lax.rem(256 - shifts[i], 256), 1)[0:1, 0:128]
            vir = jnp.broadcast_to(vir, (128, 128)).T
            vir = jnp.where(half, vir[:48], vir[48:96])
            for k in range(n):
                value = vir - occ_row[:, 128 * k : 128 * k + 128]
                if i < 2:
                    den1[i, 48 * k : 48 * k + 48, :] = value
                else:
                    den2[48 * k : 48 * k + 48, :] = value

    get_partner.wait()
    map_pairs()
    differences(amplitudes, own, get_amplitudes)
    get_mask.wait()
    pl.semaphore_wait(barrier, len(peers))

    gather_z = [None] * n
    gather_y = [[] for _ in range(n)]

    def spread_y(k, src, dst):
        for d in (2, 1, 3):
            gather_y[k].append(send(src, dst, at(y_=wrap(y + d, 4))))

    def start_gather(k):
        row, rows = CHUNKS[k]
        gat = bufs[k][0]
        mine = own.at[pl.ds(row, rows)]
        gather_z[k] = [send(mine, gat.at[y, d], at(zl_=wrap(zl + d, 4))) for d in (3, 1, 2)]
        gat[y, 0] = own[row : row + rows]
        if k not in LATE:
            spread_y(k, mine, gat.at[y, 0])

    def forward(k):
        gat = bufs[k][0]
        if k in LATE:
            for copy in gather_z[k]:
                copy.wait_recv()
            spread_y(k, gat.at[y], gat.at[y])
        else:
            for copy, d in zip(gather_z[k][1:] + gather_z[k][:1], (1, 2, 3)):
                copy.wait_recv()
                spread_y(k, gat.at[y, d], gat.at[y, d])

    def split_tile(t):
        for load in loads[t]:
            load.wait()
        pieces = []
        for p, first in enumerate(starts(t)):
            cut = min(48, W * (first // W + 1) - first)
            pieces.append((48 * p, cut, first // W))
            if cut < 48:
                pieces.append((48 * p + cut, 48 - cut, first // W + 1))

        def body(j, carry):
            cols = pl.ds(pl.multiple_of(j * W, W), W)
            for at_row, count, tile in pieces:
                v = stage[t, at_row : at_row + count, cols] * mask[tile, j].astype(jnp.float32)
                h = v.astype(jnp.bfloat16)
                rows = slice(192 * t + at_row, 192 * t + at_row + count)
                hi[rows, cols] = h
                lo[rows, cols] = (v - h.astype(jnp.float32)).astype(jnp.bfloat16)
            return carry

        lax.fori_loop(0, 6, body, 0)

    def turn_out(first, last):
        def body(t, carry):
            q = t % 4
            lanes = pl.ds(pl.multiple_of((t // 4) * W, W), W)
            cols = pl.ds(pl.multiple_of(q * 384, 384), 384)
            for src, dst in ((hi, hi_t), (lo, lo_t)):
                turned = src[lanes, cols].T
                for p in range(4):
                    for h in range(2):
                        rows = pl.ds(pl.multiple_of(768 * h + 192 * q + 48 * p, 16), 48)
                        dst[rows, lanes] = turned[96 * p + 48 * h : 96 * p + 48 * h + 48]
            return carry

        lax.fori_loop(first, last, body, 0)

    def turn_back(first, last):
        def body(t, carry):
            rows = pl.ds(pl.multiple_of((t // 6) * W, W), W)
            cols = pl.ds(pl.multiple_of((t % 6) * W, W), W)
            hi[cols, rows] = hi_t[rows, cols].T
            lo[cols, rows] = lo_t[rows, cols].T
            return carry

        lax.fori_loop(first, last, body, 0)

    def fill_left(slot, slab):
        for i in range(2):
            turned = jnp.concatenate([slab(8 * i + p) for p in range(8)], axis=0).T
            high = turned.astype(jnp.bfloat16)
            low = (turned - high.astype(jnp.float32)).astype(jnp.bfloat16)
            lanes = slice(384 * i, 384 * i + 384)
            for part in range(2):
                left[slot, part, 0:64, lanes] = high[64 * part : 64 * part + 64]
                left[slot, part, 64:128, lanes] = low[64 * part : 64 * part + 64]

    def product(slot, high, low, i):
        parts = []
        for part in range(2):
            lanes = pl.ds(pl.multiple_of(768 * part + 384 * i, 128), 384)
            both = jnp.dot(left[slot, 0], high[0:768, lanes], preferred_element_type=jnp.float32)
            both = both + jnp.dot(left[slot, 1], high[768:1536, lanes], preferred_element_type=jnp.float32)
            rest_ = jnp.dot(left[slot, 0, 0:64], low[0:768, lanes], preferred_element_type=jnp.float32)
            rest_ = rest_ + jnp.dot(left[slot, 1, 0:64], low[768:1536, lanes], preferred_element_type=jnp.float32)
            parts.append(both[0:64] + (both[64:128] + rest_))
        return jnp.concatenate(parts, axis=0).T

    core_copies = [None] * n

    def first_product(k):
        gat, par, corr = bufs[k][0], bufs[k][1], bufs[k][2]
        for copy in gather_y[k]:
            copy.wait_recv()
        fill_left(k, lambda b: gat[b // 4, wrap(zl - b % 4 + 4, 4)])
        base = take(2)

        def core_copy(i):
            return describe(base + i, par.at[1 - c, i], corr.at[i], at(c_=1 - c))

        def body(i, carry):
            packed = product(k, hi_t, lo_t, i)
            for p in range(8):
                par[p % 2, i, p // 2] = packed[48 * p : 48 * p + 48]
            core_copy(i).start()
            return carry

        lax.fori_loop(0, 2, body, 0)
        core_copies[k] = [core_copy(i) for i in range(2)]
        sent.extend(core_copies[k])

    x_copies = [None] * n

    def reduce_x(k):
        par, corr, xsum, xrecv = bufs[k][1], bufs[k][2], bufs[k][3], bufs[k][4]
        for copy in core_copies[k]:
            copy.wait_recv()
        x_copies[k] = []
        for d in (2, 1, 3, 0):
            xd = wrap(x + d, 4)
            for h in range(2):
                xsum[xd, h] = par[c, h, xd] + corr[h, xd]
            if d:
                x_copies[k].append(send(xsum.at[xd], xrecv.at[d - 1], at(x_=xd)))

    h_copies = [None] * n

    def reduce_h(k):
        xsum, xrecv, hsum, hrecv = bufs[k][3], bufs[k][4], bufs[k][5], bufs[k][6]
        for copy in x_copies[k]:
            copy.wait_recv()
        for h in range(2):
            hsum[h] = (xsum[x, h] + xrecv[1, h]) + (xrecv[0, h] + xrecv[2, h])
        h_copies[k] = send(hsum, hrecv, at(zh_=1 - zh))

    ux_copies = [None] * n
    uc_copies = [None] * n

    def forward_core(k, first, count):
        ug = bufs[k][7]
        piece = ug.at[c, pl.ds(first, count)]
        uc_copies[k].append(send(piece, piece, at(c_=1 - c)))

    def update_one(k):
        row, rows = CHUNKS[k]
        hsum, hrecv, ug = bufs[k][5], bufs[k][6], bufs[k][7]
        h_copies[k].wait_recv()
        here = slice(row, row + rows)
        both = []
        for h in range(2):
            other = jnp.where(zh == h, oth1[here, :], oth1_peer[here, :])
            value = (other + (hsum[h] + hrecv[h])) / den1[h, here, :]
            ug[c, 0, h] = value
            both.append(value)
        ux_copies[k] = []
        uc_copies[k] = []
        for d in (2, 1, 3):
            ux_copies[k].append(send(ug.at[c, 0], ug.at[c, d], at(x_=wrap(x + d, 4))))
        forward_core(k, 0, 1)
        new1[here, :] = jnp.where(zh == 0, both[0], both[1])

    def pass_core(k):
        for copy in ux_copies[k]:
            copy.wait_recv()
        forward_core(k, 1, 3)

    y_copies = [None] * n

    def second_product(k):
        ug, par, yrecv = bufs[k][7], bufs[k][8], bufs[k][9]
        for copy in uc_copies[k]:
            copy.wait_recv()
        fill_left(3 + k, lambda b: ug[b % 2, wrap(x - (b // 2) % 4 + 4, 4), b // 8])
        base = take(3)

        def y_copy(yd, d):
            return describe(base + d - 1, par.at[yd], yrecv.at[d - 1], at(y_=yd))

        def body(i, carry):
            packed = product(3 + k, hi, lo, i)
            for p in range(8):
                par[2 * i + p // 4, p % 4] = packed[48 * p : 48 * p + 48]
            for e in range(2):
                yd = 2 * i + e
                d = lax.rem(yd - y + 4, 4)

                @pl.when(d > 0)
                def _():
                    y_copy(yd, d).start()

            return carry

        lax.fori_loop(0, 2, body, 0)
        y_copies[k] = [y_copy(wrap(y + d, 4), d) for d in (1, 2, 3)]
        sent.extend(y_copies[k])

    l_copies = [None] * n

    def reduce_l(k):
        par, yrecv, ysum, lrecv = bufs[k][8], bufs[k][9], bufs[k][10], bufs[k][11]
        for copy in y_copies[k]:
            copy.wait_recv()
        l_copies[k] = []
        for d in (2, 1, 3, 0):
            ld = wrap(zl + d, 4)
            ysum[ld] = (par[y, ld] + yrecv[0, ld]) + (yrecv[1, ld] + yrecv[2, ld])
            if d:
                l_copies[k].append(send(ysum.at[ld], lrecv.at[d - 1], at(zl_=ld)))

    def update_two(k):
        row, rows = CHUNKS[k]
        ysum, lrecv = bufs[k][10], bufs[k][11]
        for copy in l_copies[k]:
            copy.wait_recv()
        here = slice(row, row + rows)
        ladder = (ysum[zl] + lrecv[0]) + (lrecv[1] + lrecv[2])
        new2[here, :] = (oth2[here, :] + ladder) / den2[here, :]

    start_gather(0)
    start_gather(1)
    split_tile(0)
    split_tile(1)
    split_tile(2)
    split_tile(3)
    forward(0)
    start_gather(2)
    split_tile(4)
    split_tile(5)
    forward(1)
    split_tile(6)
    split_tile(7)
    turn_out(0, 24)
    forward(2)
    differences(other_first, oth1, get_first)
    other_copy = send(oth1, oth1_peer, at(zh_=1 - zh))
    first_product(0)
    denominators()
    reduce_x(0)
    first_product(1)
    reduce_h(0)
    reduce_x(1)
    first_product(2)
    turn_back(0, 18)
    differences(other_second, oth2, get_second)
    other_copy.wait_recv()
    update_one(0)
    reduce_h(1)
    reduce_x(2)
    turn_back(18, 36)
    pass_core(0)
    update_one(1)
    reduce_h(2)
    second_product(0)
    pass_core(1)
    update_one(2)
    second_product(1)
    pass_core(2)
    reduce_l(0)
    expand(new1, result1, 0, 3)
    second_product(2)
    reduce_l(1)
    update_two(0)
    reduce_l(2)
    update_two(1)
    expand(new2, result2, 0, 2)
    update_two(2)
    expand(new2, result2, 2, 3)
    for copy in sent:
        copy.wait_send()


def per_device(
    integrals,
    tile_mask,
    amplitudes,
    other_first,
    other_second,
    vir_index,
    occ_index,
    partner,
    eps_vir,
    eps_occ,
):
    f32, bf16 = jnp.float32, jnp.bfloat16
    side = integrals.shape[0]
    packed = (144, 128)
    scratch = [pltpu.VMEM((8, 192, side), f32)]
    scratch += [pltpu.VMEM((side, side), bf16)] * 4
    scratch += [pltpu.VMEM((6, 2, 128, side // 2), bf16)]
    scratch += [pltpu.VMEM(packed, f32)] * 4
    scratch += [pltpu.VMEM((2,) + packed, f32)]
    scratch += [pltpu.VMEM(packed, f32)] * 3
    scratch += [pltpu.VMEM((384, 384), bf16), pltpu.VMEM((3, 2, 256), jnp.int32)]
    scratch += [pltpu.SMEM(tile_mask.shape, jnp.int32)] + [pltpu.VMEM(amplitudes.shape, f32)] * 3
    scratch += [pltpu.VMEM(occ_index.shape, jnp.int32), pltpu.VMEM((1,) + partner.shape, jnp.int32)]
    scratch += [pltpu.VMEM((1,) + eps_vir.shape, f32), pltpu.SMEM(eps_occ.shape, f32)]
    for _, rows in CHUNKS:
        for lead in (
            (4, 4), (2, 2, 4), (2, 4), (4, 2), (3, 2), (2,), (2,), (2, 4, 2), (4, 4), (3, 4), (4,), (3,)
        ):
            scratch.append(pltpu.VMEM(lead + (rows, 128), f32))
    scratch += [
        pltpu.SemaphoreType.DMA((8, 4)),
        pltpu.SemaphoreType.DMA((3,)),
        pltpu.SemaphoreType.DMA((10,)),
        pltpu.SemaphoreType.DMA((N_SEMS,)),
        pltpu.SemaphoreType.DMA((N_SEMS,)),
    ]
    hbm = pl.BlockSpec(memory_space=pl.ANY)
    shapes = [jax.ShapeDtypeStruct(amplitudes.shape, f32)] * 2
    return pl.pallas_call(
        ladder_kernel,
        out_shape=shapes,
        in_specs=[hbm] * 10,
        out_specs=[pl.BlockSpec(memory_space=pltpu.VMEM)] * 2,
        scratch_shapes=scratch,
        compiler_params=pltpu.CompilerParams(
            collective_id=0, has_side_effects=True, vmem_limit_bytes=53 * 1024 * 1024
        ),
        name="ladders",
    )(
        *(
            pltpu.with_memory_space_constraint(value, pltpu.HBM)
            for value in (
                integrals, tile_mask, amplitudes, other_first, other_second,
                vir_index, occ_index, partner, eps_vir, eps_occ,
            )
        )
    )


def solution(mesh):
    return jax.shard_map(
        per_device,
        mesh=mesh,
        in_specs=(
            P("res", "con"),
            P("res", "con"),
            P(("con", "res"), None),
            P(("res", "con"), None),
            P(("con", "res"), None),
            P(),
            P(),
            P(),
            P(),
            P(),
        ),
        out_specs=(P(("res", "con"), None), P(("con", "res"), None)),
        check_vma=False,
    )
```

```python
import jax
import jax.numpy as jnp
from jax import lax
from jax.experimental import pallas as pl
from jax.experimental.pallas import tpu as pltpu
from jax.sharding import PartitionSpec as P

W = 256
MESH = pl.DeviceIdType.MESH

N_X, N_C, N_H, N_Y, N_L = 4, 2, 2, 4, 4
CHUNKS = ((0, 48), (48, 48), (96, 48))
N_SEMS = 128
LATE = (1, 2)


def split_three(v):
    one = v.astype(jnp.bfloat16)
    v = v - one.astype(jnp.float32)
    two = v.astype(jnp.bfloat16)
    three = (v - two.astype(jnp.float32)).astype(jnp.bfloat16)
    return jnp.concatenate([one, two, three], axis=0)


def join_three(v):
    n = v.shape[0] // 3
    return (v[2 * n :] + v[n : 2 * n]) + v[:n]


def ladder_kernel(
    integrals, mask_in, amplitudes_in, first_in, second_in, vir_index, occ_in, partner_in, vir_in, eps_occ_in,
    result1, result2, stage, hi, lo, hi_t, lo_t, left, own, oth1, oth1_peer, oth2, den1, den2, new1,
    new2, pairs, window, mask, amplitudes, other_first, other_second, occ_index, partner, eps_vir, eps_occ, *rest
):
    n = len(CHUNKS)
    per = 12
    bufs = [rest[per * k : per * k + per] for k in range(n)]
    stage_sem, window_sem, small_sem, ssem, rsem = rest[per * n :]
    con = lax.axis_index("con")
    res = lax.axis_index("res")
    zh, x, c = con // 8, (con // 2) % 4, con % 2
    y, zl = res // 4, res % 4

    def wrap(v, m):
        return lax.rem(v + m, m)

    def at(zh_=None, x_=None, c_=None, y_=None, zl_=None):
        zh_ = zh if zh_ is None else zh_
        x_ = x if x_ is None else x_
        c_ = c if c_ is None else c_
        y_ = y if y_ is None else y_
        zl_ = zl if zl_ is None else zl_
        return (zh_ * 8 + x_ * 2 + c_, y_ * 4 + zl_)

    used = [0]
    sent = []

    def take(count):
        first = used[0]
        used[0] += count
        return first

    def describe(index, src, dst, device):
        return pltpu.make_async_remote_copy(
            src_ref=src, dst_ref=dst, send_sem=ssem.at[index], recv_sem=rsem.at[index],
            device_id=device, device_id_type=MESH,
        )

    def send(src, dst, device):
        copy = describe(take(1), src, dst, device)
        copy.start()
        sent.append(copy)
        return copy

    peers = (
        [at(zl_=wrap(zl + d, 4)) for d in (1, 2, 3)]
        + [at(y_=wrap(y + d, 4)) for d in (1, 2, 3)]
        + [at(x_=wrap(x + d, 4)) for d in (1, 2, 3)]
        + [at(c_=1 - c), at(zh_=1 - zh)]
    )
    barrier = pltpu.get_barrier_semaphore()
    for peer in peers:
        pl.semaphore_signal(barrier, inc=1, device_id=peer, device_id_type=MESH)

    def bring(i, src, dst):
        copy = pltpu.make_async_copy(src, dst, small_sem.at[i])
        copy.start()
        return copy

    get_partner = bring(0, partner_in, partner.at[0])
    get_amplitudes = bring(1, amplitudes_in, amplitudes)
    get_mask = bring(2, mask_in, mask)
    def starts(t):
        return [96 * (4 * (t % 4) + p) + 48 * (t // 4) for p in range(4)]

    loads = [
        [
            pltpu.make_async_copy(
                integrals.at[pl.ds(first, 48)], stage.at[t, pl.ds(48 * p, 48)], stage_sem.at[t, p]
            )
            for p, first in enumerate(starts(t))
        ]
        for t in range(8)
    ]
    for group in loads:
        for load in group:
            load.start()
    get_first = bring(3, first_in, other_first)
    get_second = bring(4, second_in, other_second)
    get_energies = [
        bring(5, occ_in, occ_index), bring(6, vir_in, eps_vir.at[0]), bring(7, eps_occ_in, eps_occ)
    ]
    blocks = (res * 16 + con % 8, res * 16 + 8 + con % 8, con * 16 + res)
    shifts, windows = [], []
    for i, block in enumerate(blocks):
        first = lax.min(block * 96 // 128 * 128, vir_index.shape[1] - 256)
        first = pl.multiple_of(first, 128)
        shifts.append(block * 96 - first)
        windows.append(
            pltpu.make_async_copy(vir_index.at[:, pl.ds(first, 256)], window.at[i], window_sem.at[i])
        )
        windows[i].start()

    half = lax.broadcasted_iota(jnp.int32, (48, 128), 1) < 64

    def map_pairs():
        size = partner.shape[1]
        row = partner[...].astype(jnp.float32)
        col = jnp.broadcast_to(row, (128, size)).T
        col = jnp.concatenate([col] * (size // 128), axis=1)
        down = lax.broadcasted_iota(jnp.int32, (size, size), 0).astype(jnp.float32)
        across = lax.broadcasted_iota(jnp.int32, (size, size), 1)
        wide = across.astype(jnp.float32)
        before = (wide < jnp.minimum(down, col)) & (wide < jnp.broadcast_to(row, (size, size)))
        before = jnp.where(before, 1.0, 0.0).astype(jnp.bfloat16)
        couple = jnp.dot(before, jnp.ones((size, size), jnp.bfloat16), preferred_element_type=jnp.float32)
        place = (64 * (across // 128) + across % 64).astype(jnp.float32)
        sign = jnp.where(down < col, 1.0, -1.0)
        pairs[...] = jnp.where(couple == place, sign, 0.0).astype(jnp.bfloat16)

    def differences(src, dst, copy):
        copy.wait()
        wide = join_three(jnp.dot(split_three(src[...]), pairs[...], preferred_element_type=jnp.float32))
        for k in range(n):
            part = wide[:, 128 * k : 128 * k + 128]
            dst[48 * k : 48 * k + 48, :] = jnp.where(half, part[:48], part[48:])

    def expand(src, dst, first, last):
        parts = [src[48 * k : 48 * k + 48, :] for k in range(first, last)]
        top = jnp.concatenate([jnp.where(half, part, 0.0) for part in parts], axis=1)
        bottom = jnp.concatenate([jnp.where(half, 0.0, part) for part in parts], axis=1)
        both = split_three(0.5 * jnp.concatenate([top, bottom], axis=0))
        value = join_three(
            lax.dot_general(
                both,
                pairs[:, 128 * first : 128 * last],
                (((1,), (1,)), ((), ())),
                preferred_element_type=jnp.float32,
            )
        )
        dst[...] = value if first == 0 else dst[...] + value

    def denominators():
        for copy in get_energies:
            copy.wait()
        occ = occ_index[...]
        picked = jnp.zeros(occ.shape, jnp.float32)
        for i in range(eps_occ.shape[0]):
            picked = jnp.where(occ == i, eps_occ[i], picked)
        energy = jnp.broadcast_to(picked[0:1] + picked[1:2], (16, occ.shape[1]))
        firsts = jnp.maximum(pairs[...].astype(jnp.float32), 0.0).astype(jnp.bfloat16)
        occ_row = join_three(jnp.dot(split_three(energy), firsts, preferred_element_type=jnp.float32))[0:1]
        table = split_three(jnp.broadcast_to(eps_vir[...], (16, eps_vir.shape[1])))
        orbitals = lax.broadcasted_iota(jnp.int32, (eps_vir.shape[1], 256), 0)
        for i in range(3):
            windows[i].wait()
            found = window[i]
            counts = jnp.where(orbitals == found[0:1], 1.0, 0.0) + jnp.where(orbitals == found[1:2], 1.0, 0.0)
            vir = join_three(jnp.dot(table, counts.astype(jnp.bfloat16), preferred_element_type=jnp.float32))
            vir = pltpu.roll(vir, lax.rem(256 - shifts[i], 256), 1)[0:1, 0:128]
            vir = jnp.broadcast_to(vir, (128, 128)).T
            vir = jnp.where(half, vir[:48], vir[48:96])
            for k in range(n):
                value = vir - occ_row[:, 128 * k : 128 * k + 128]
                if i < 2:
                    den1[i, 48 * k : 48 * k + 48, :] = value
                else:
                    den2[48 * k : 48 * k + 48, :] = value

    get_partner.wait()
    map_pairs()
    differences(amplitudes, own, get_amplitudes)
    get_mask.wait()
    pl.semaphore_wait(barrier, len(peers))

    gather_z = [None] * n
    gather_y = [[] for _ in range(n)]

    def spread_y(k, src, dst):
        for d in (2, 1, 3):
            gather_y[k].append(send(src, dst, at(y_=wrap(y + d, 4))))

    def start_gather(k):
        row, rows = CHUNKS[k]
        gat = bufs[k][0]
        mine = own.at[pl.ds(row, rows)]
        gather_z[k] = [send(mine, gat.at[y, d], at(zl_=wrap(zl + d, 4))) for d in (3, 1, 2)]
        gat[y, 0] = own[row : row + rows]
        if k not in LATE:
            spread_y(k, mine, gat.at[y, 0])

    def forward(k):
        gat = bufs[k][0]
        if k in LATE:
            for copy in gather_z[k]:
                copy.wait_recv()
            spread_y(k, gat.at[y], gat.at[y])
        else:
            for copy, d in zip(gather_z[k][1:] + gather_z[k][:1], (1, 2, 3)):
                copy.wait_recv()
                spread_y(k, gat.at[y, d], gat.at[y, d])

    def split_tile(t):
        for load in loads[t]:
            load.wait()
        pieces = []
        for p, first in enumerate(starts(t)):
            cut = min(48, W * (first // W + 1) - first)
            pieces.append((48 * p, cut, first // W))
            if cut < 48:
                pieces.append((48 * p + cut, 48 - cut, first // W + 1))

        def body(j, carry):
            cols = pl.ds(pl.multiple_of(j * W, W), W)
            for at_row, count, tile in pieces:
                v = stage[t, at_row : at_row + count, cols] * mask[tile, j].astype(jnp.float32)
                h = v.astype(jnp.bfloat16)
                rows = slice(192 * t + at_row, 192 * t + at_row + count)
                hi[rows, cols] = h
                lo[rows, cols] = (v - h.astype(jnp.float32)).astype(jnp.bfloat16)
            return carry

        lax.fori_loop(0, 6, body, 0)

    def turn_out(first, last):
        def body(t, carry):
            q = t % 4
            lanes = pl.ds(pl.multiple_of((t // 4) * W, W), W)
            cols = pl.ds(pl.multiple_of(q * 384, 384), 384)
            for src, dst in ((hi, hi_t), (lo, lo_t)):
                turned = src[lanes, cols].T
                for p in range(4):
                    for h in range(2):
                        rows = pl.ds(pl.multiple_of(768 * h + 192 * q + 48 * p, 16), 48)
                        dst[rows, lanes] = turned[96 * p + 48 * h : 96 * p + 48 * h + 48]
            return carry

        lax.fori_loop(first, last, body, 0)

    def turn_back(first, last):
        def body(t, carry):
            rows = pl.ds(pl.multiple_of((t // 6) * W, W), W)
            cols = pl.ds(pl.multiple_of((t % 6) * W, W), W)
            hi[cols, rows] = hi_t[rows, cols].T
            lo[cols, rows] = lo_t[rows, cols].T
            return carry

        lax.fori_loop(first, last, body, 0)

    def fill_left(slot, slab):
        for i in range(2):
            turned = jnp.concatenate([slab(8 * i + p) for p in range(8)], axis=0).T
            high = turned.astype(jnp.bfloat16)
            low = (turned - high.astype(jnp.float32)).astype(jnp.bfloat16)
            lanes = slice(384 * i, 384 * i + 384)
            for part in range(2):
                left[slot, part, 0:64, lanes] = high[64 * part : 64 * part + 64]
                left[slot, part, 64:128, lanes] = low[64 * part : 64 * part + 64]

    def product(slot, high, low, i):
        parts = []
        for part in range(2):
            lanes = pl.ds(pl.multiple_of(768 * part + 384 * i, 128), 384)
            both = jnp.dot(left[slot, 0], high[0:768, lanes], preferred_element_type=jnp.float32)
            both = both + jnp.dot(left[slot, 1], high[768:1536, lanes], preferred_element_type=jnp.float32)
            rest_ = jnp.dot(left[slot, 0, 0:64], low[0:768, lanes], preferred_element_type=jnp.float32)
            rest_ = rest_ + jnp.dot(left[slot, 1, 0:64], low[768:1536, lanes], preferred_element_type=jnp.float32)
            parts.append(both[0:64] + (both[64:128] + rest_))
        return jnp.concatenate(parts, axis=0).T

    core_copies = [None] * n

    def first_product(k):
        gat, par, corr = bufs[k][0], bufs[k][1], bufs[k][2]
        for copy in gather_y[k]:
            copy.wait_recv()
        fill_left(k, lambda b: gat[b // 4, wrap(zl - b % 4 + 4, 4)])
        base = take(2)

        def core_copy(i):
            return describe(base + i, par.at[1 - c, i], corr.at[i], at(c_=1 - c))

        def body(i, carry):
            packed = product(k, hi_t, lo_t, i)
            for p in range(8):
                par[p % 2, i, p // 2] = packed[48 * p : 48 * p + 48]
            core_copy(i).start()
            return carry

        lax.fori_loop(0, 2, body, 0)
        core_copies[k] = [core_copy(i) for i in range(2)]
        sent.extend(core_copies[k])

    x_copies = [None] * n

    def reduce_x(k):
        par, corr, xsum, xrecv = bufs[k][1], bufs[k][2], bufs[k][3], bufs[k][4]
        for copy in core_copies[k]:
            copy.wait_recv()
        x_copies[k] = []
        for d in (2, 1, 3, 0):
            xd = wrap(x + d, 4)
            for h in range(2):
                xsum[xd, h] = par[c, h, xd] + corr[h, xd]
            if d:
                x_copies[k].append(send(xsum.at[xd], xrecv.at[d - 1], at(x_=xd)))

    h_copies = [None] * n

    def reduce_h(k):
        xsum, xrecv, hsum, hrecv = bufs[k][3], bufs[k][4], bufs[k][5], bufs[k][6]
        for copy in x_copies[k]:
            copy.wait_recv()
        for h in range(2):
            hsum[h] = (xsum[x, h] + xrecv[1, h]) + (xrecv[0, h] + xrecv[2, h])
        h_copies[k] = send(hsum, hrecv, at(zh_=1 - zh))

    ux_copies = [None] * n
    uc_copies = [None] * n

    def forward_core(k, first, count):
        ug = bufs[k][7]
        piece = ug.at[c, pl.ds(first, count)]
        uc_copies[k].append(send(piece, piece, at(c_=1 - c)))

    def update_one(k):
        row, rows = CHUNKS[k]
        hsum, hrecv, ug = bufs[k][5], bufs[k][6], bufs[k][7]
        h_copies[k].wait_recv()
        here = slice(row, row + rows)
        both = []
        for h in range(2):
            other = jnp.where(zh == h, oth1[here, :], oth1_peer[here, :])
            value = (other + (hsum[h] + hrecv[h])) / den1[h, here, :]
            ug[c, 0, h] = value
            both.append(value)
        ux_copies[k] = []
        uc_copies[k] = []
        for d in (2, 1, 3):
            ux_copies[k].append(send(ug.at[c, 0], ug.at[c, d], at(x_=wrap(x + d, 4))))
        forward_core(k, 0, 1)
        new1[here, :] = jnp.where(zh == 0, both[0], both[1])

    def pass_core(k):
        for copy in ux_copies[k]:
            copy.wait_recv()
        forward_core(k, 1, 3)

    y_copies = [None] * n

    def second_product(k):
        ug, par, yrecv = bufs[k][7], bufs[k][8], bufs[k][9]
        for copy in uc_copies[k]:
            copy.wait_recv()
        fill_left(3 + k, lambda b: ug[b % 2, wrap(x - (b // 2) % 4 + 4, 4), b // 8])
        base = take(3)

        def y_copy(yd, d):
            return describe(base + d - 1, par.at[yd], yrecv.at[d - 1], at(y_=yd))

        def body(i, carry):
            packed = product(3 + k, hi, lo, i)
            for p in range(8):
                par[2 * i + p // 4, p % 4] = packed[48 * p : 48 * p + 48]
            for e in range(2):
                yd = 2 * i + e
                d = lax.rem(yd - y + 4, 4)

                @pl.when(d > 0)
                def _():
                    y_copy(yd, d).start()

            return carry

        lax.fori_loop(0, 2, body, 0)
        y_copies[k] = [y_copy(wrap(y + d, 4), d) for d in (1, 2, 3)]
        sent.extend(y_copies[k])

    l_copies = [None] * n

    def reduce_l(k):
        par, yrecv, ysum, lrecv = bufs[k][8], bufs[k][9], bufs[k][10], bufs[k][11]
        for copy in y_copies[k]:
            copy.wait_recv()
        l_copies[k] = []
        for d in (2, 1, 3, 0):
            ld = wrap(zl + d, 4)
            ysum[ld] = (par[y, ld] + yrecv[0, ld]) + (yrecv[1, ld] + yrecv[2, ld])
            if d:
                l_copies[k].append(send(ysum.at[ld], lrecv.at[d - 1], at(zl_=ld)))

    def update_two(k):
        row, rows = CHUNKS[k]
        ysum, lrecv = bufs[k][10], bufs[k][11]
        for copy in l_copies[k]:
            copy.wait_recv()
        here = slice(row, row + rows)
        ladder = (ysum[zl] + lrecv[0]) + (lrecv[1] + lrecv[2])
        new2[here, :] = (oth2[here, :] + ladder) / den2[here, :]

    start_gather(0)
    start_gather(1)
    split_tile(0)
    split_tile(1)
    split_tile(2)
    split_tile(3)
    forward(0)
    start_gather(2)
    split_tile(4)
    split_tile(5)
    forward(1)
    split_tile(6)
    split_tile(7)
    turn_out(0, 24)
    forward(2)
    differences(other_first, oth1, get_first)
    other_copy = send(oth1, oth1_peer, at(zh_=1 - zh))
    first_product(0)
    reduce_x(0)
    first_product(1)
    reduce_h(0)
    reduce_x(1)
    first_product(2)
    denominators()
    other_copy.wait_recv()
    update_one(0)
    reduce_h(1)
    reduce_x(2)
    turn_back(0, 36)
    differences(other_second, oth2, get_second)
    pass_core(0)
    update_one(1)
    reduce_h(2)
    second_product(0)
    pass_core(1)
    update_one(2)
    second_product(1)
    pass_core(2)
    reduce_l(0)
    expand(new1, result1, 0, 3)
    second_product(2)
    reduce_l(1)
    update_two(0)
    reduce_l(2)
    update_two(1)
    expand(new2, result2, 0, 2)
    update_two(2)
    expand(new2, result2, 2, 3)
    for copy in sent:
        copy.wait_send()


def per_device(
    integrals,
    tile_mask,
    amplitudes,
    other_first,
    other_second,
    vir_index,
    occ_index,
    partner,
    eps_vir,
    eps_occ,
):
    f32, bf16 = jnp.float32, jnp.bfloat16
    side = integrals.shape[0]
    packed = (144, 128)
    scratch = [pltpu.VMEM((8, 192, side), f32)]
    scratch += [pltpu.VMEM((side, side), bf16)] * 4
    scratch += [pltpu.VMEM((6, 2, 128, side // 2), bf16)]
    scratch += [pltpu.VMEM(packed, f32)] * 4
    scratch += [pltpu.VMEM((2,) + packed, f32)]
    scratch += [pltpu.VMEM(packed, f32)] * 3
    scratch += [pltpu.VMEM((384, 384), bf16), pltpu.VMEM((3, 2, 256), jnp.int32)]
    scratch += [pltpu.SMEM(tile_mask.shape, jnp.int32)] + [pltpu.VMEM(amplitudes.shape, f32)] * 3
    scratch += [pltpu.VMEM(occ_index.shape, jnp.int32), pltpu.VMEM((1,) + partner.shape, jnp.int32)]
    scratch += [pltpu.VMEM((1,) + eps_vir.shape, f32), pltpu.SMEM(eps_occ.shape, f32)]
    for _, rows in CHUNKS:
        for lead in (
            (4, 4), (2, 2, 4), (2, 4), (4, 2), (3, 2), (2,), (2,), (2, 4, 2), (4, 4), (3, 4), (4,), (3,)
        ):
            scratch.append(pltpu.VMEM(lead + (rows, 128), f32))
    scratch += [
        pltpu.SemaphoreType.DMA((8, 4)),
        pltpu.SemaphoreType.DMA((3,)),
        pltpu.SemaphoreType.DMA((10,)),
        pltpu.SemaphoreType.DMA((N_SEMS,)),
        pltpu.SemaphoreType.DMA((N_SEMS,)),
    ]
    hbm = pl.BlockSpec(memory_space=pl.ANY)
    shapes = [jax.ShapeDtypeStruct(amplitudes.shape, f32)] * 2
    return pl.pallas_call(
        ladder_kernel,
        out_shape=shapes,
        in_specs=[hbm] * 10,
        out_specs=[pl.BlockSpec(memory_space=pltpu.VMEM)] * 2,
        scratch_shapes=scratch,
        compiler_params=pltpu.CompilerParams(
            collective_id=0, has_side_effects=True, vmem_limit_bytes=53 * 1024 * 1024
        ),
        name="ladders",
    )(
        *(
            pltpu.with_memory_space_constraint(value, pltpu.HBM)
            for value in (
                integrals, tile_mask, amplitudes, other_first, other_second,
                vir_index, occ_index, partner, eps_vir, eps_occ,
            )
        )
    )


def solution(mesh):
    return jax.shard_map(
        per_device,
        mesh=mesh,
        in_specs=(
            P("res", "con"),
            P("res", "con"),
            P(("con", "res"), None),
            P(("res", "con"), None),
            P(("con", "res"), None),
            P(),
            P(),
            P(),
            P(),
            P(),
        ),
        out_specs=(P(("res", "con"), None), P(("con", "res"), None)),
        check_vma=False,
    )
```
